128 devices in a mesh: res: 32 (over z, y, core), col: 4 (over x).
Axes of the slice: x: 4, y: 4, z: 4, core: 2. Of those that a mesh axis runs over, the one named last changes fastest.
Arguments:
- homolog_embedding: bfloat16 [128, 1536, 256], P('res', 'col'), may hold values from -6 to 6
- sequence_row_mask: bfloat16 [128, 8], P('res'), may hold values from 0 to 1, as said below
- residue_chain_index: int32 [1536], P('col'), may hold values from 0 to 7, never falling along the last dimension, each value on 1 to 384 neighbouring positions
- standardize_factor: float32 [256], replicated, may hold values from 0.1 to 1.9
- standardize_shift: float32 [256], replicated, may hold values from -3 to 3
- first_projector_matrix: bfloat16 [256, 32], replicated, may hold values from -0.375 to 0.375
- second_projector_matrix: bfloat16 [256, 32], replicated, may hold values from -0.375 to 0.375
- output_weight: bfloat16 [1024, 128], replicated, may hold values from -1 to 1
Outputs:
- pair_update: bfloat16 [1536, 1536, 128], P('res', 'col')
The draws below stay inside these ranges and needn't reach their ends.
Inputs may be any that keep to these rules, and one draw needn't show every extreme that they name: `sequence_row_mask`: row 0 is all ones. `residue_chain_index`: chain numbers never fall along the residues.
All inputs are finite; a program needn't handle non-finite values.
Results may differ from the reference program's by a relative error of at most 0.0063.
Values may be sent and summed in bfloat16 or wider, within the bound.
No kernel may reach another device: no remote copies, remote signals or barrier semaphores. Data moves between devices by JAX's collectives and lax.ppermute only.
A program may use at most 192 MiB of HBM per device.

```python
import math
import jax
import jax.numpy as jnp
import numpy as np
from jax import lax

EMBED_DEPTH = 256
HIDDEN_PER_SIDE = 32
C_Z = 128
CHAINS = 8
HOMOLOG_COUNT = 128
AMINO_COUNT = 1536


def draw_sequence_row_mask(key, part):
    key = jax.random.fold_in(key, 11)
    pick_key, level_key = jax.random.split(key)
    values = jax.random.randint(pick_key, (HOMOLOG_COUNT, CHAINS), 0, 1000)
    ceiling = 250 + 700 * jnp.arange(HOMOLOG_COUNT, dtype=jnp.int32) // max(HOMOLOG_COUNT - 1, 1)
    picked = (values < ceiling[:, None]).astype(jnp.float32)
    levels = jax.random.uniform(level_key, (HOMOLOG_COUNT, CHAINS), jnp.float32, 0.1, 1.0)
    weights = (picked * levels).at[0].set(1.0)
    return weights.astype(jnp.bfloat16)


def steps_of(key, extent, cuts, least, high):
    def one(axis_at, blocks):
        draws = jax.random.uniform(jax.random.fold_in(jax.random.fold_in(key, 6), axis_at), (blocks,), jnp.float32, least / len(cuts), high / len(cuts))
        return jnp.repeat(jnp.exp(draws), extent[axis_at] // blocks).reshape((-1,) + (1,) * (len(extent) - axis_at - 1))

    factor_of = one(*cuts[0])
    for cut in cuts[1:]:
        factor_of = factor_of * one(*cut)
    return factor_of


def profile(amount, total, reach, lean):
    portions = [(1 << 20) // math.isqrt(rank ** lean) + 1 for rank in range(2, amount + 1)]
    rest, given = total - reach - (amount - 1), [1] * (amount - 1)
    while rest > 0:
        candidates = [i for i in range(amount - 1) if given[i] < reach]
        whole, budget = sum([portions[i] for i in candidates]), rest
        for i in candidates:
            more = min(reach - given[i], max(1, budget * portions[i] // whole), rest)
            given[i] = given[i] + more
            rest = rest - more
    return np.array([reach] + given)


def ragged(stream_key, amount, total, reach, slope):
    if amount == 2:
        one = jax.random.randint(stream_key, (), max(1, total - reach), min(reach, total - 1) + 1)
        return jnp.stack([one, total - one])
    lengths = jnp.asarray(profile(amount, total, reach, slope), jnp.int32)
    twos = (amount - 1) // 2
    source_of, taker = lengths[1:1 + 2 * twos:2], lengths[2:2 + 2 * twos:2]
    slack = jnp.minimum(source_of - 1, reach - taker)
    passed = jax.random.randint(jax.random.fold_in(stream_key, 1), (twos,), 0, 1 << 20) % (slack + 1)
    lengths = lengths.at[1:1 + 2 * twos:2].set(source_of - passed).at[2:2 + 2 * twos:2].set(taker + passed)
    return lengths[jax.random.permutation(jax.random.fold_in(stream_key, 2), amount)]


def scatter_about(key, extent, deviation, most, pieces=(), kind=jnp.bfloat16):
    result = deviation * jax.random.normal(key, extent, jnp.float32)
    if pieces:
        result = result * steps_of(key, extent, pieces, -0.22, 0.18)
    return jnp.clip(result, -most, most).astype(kind)


def setup_inputs(seed: int = 0) -> dict:
    seeds = jax.random.split(jax.random.key(seed), 9)
    homolog_embedding = scatter_about(seeds[0], (HOMOLOG_COUNT, AMINO_COUNT, EMBED_DEPTH), 1.0, 6.0, ((0, 32), (1, 4)))
    sequence_row_mask = draw_sequence_row_mask(jax.random.fold_in(seeds[8], 71), 0)
    residue_chain_index = jnp.searchsorted(jnp.cumsum(ragged(seeds[2], CHAINS, AMINO_COUNT, AMINO_COUNT // 4, 2)), jnp.arange(AMINO_COUNT), side="right").astype(jnp.int32)
    standardize_factor = jnp.clip(1.0 + 0.18 * jax.random.normal(seeds[3], (EMBED_DEPTH,), jnp.float32), 0.1, 1.9)
    standardize_shift = scatter_about(seeds[4], (EMBED_DEPTH,), 0.5, 3.0, (), jnp.float32)
    first_projector_matrix = scatter_about(seeds[5], (EMBED_DEPTH, HIDDEN_PER_SIDE), EMBED_DEPTH ** -0.5, 0.375)
    second_projector_matrix = scatter_about(seeds[6], (EMBED_DEPTH, HIDDEN_PER_SIDE), EMBED_DEPTH ** -0.5, 0.375)
    output_weight = scatter_about(seeds[7], (HIDDEN_PER_SIDE * HIDDEN_PER_SIDE, C_Z), (HIDDEN_PER_SIDE * HIDDEN_PER_SIDE * 4 // HOMOLOG_COUNT) ** -0.5, 1.0)
    return {"homolog_embedding": homolog_embedding, "sequence_row_mask": sequence_row_mask, "residue_chain_index": residue_chain_index, "standardize_factor": standardize_factor, "standardize_shift": standardize_shift, "first_projector_matrix": first_projector_matrix, "second_projector_matrix": second_projector_matrix, "output_weight": output_weight}


def apply_layer_norm(feats, standardize_factor, standardize_shift):
    wide = feats.astype(jnp.float32)
    centre = lax.optimization_barrier(jnp.mean(wide, axis=-1, keepdims=True))
    shifted = wide - centre
    variance = lax.optimization_barrier(jnp.mean(shifted * shifted, axis=-1, keepdims=True))
    return shifted * lax.rsqrt(variance + 1e-05) * standardize_factor + standardize_shift

def reference(homolog_embedding, sequence_row_mask, residue_chain_index, standardize_factor, standardize_shift, first_projector_matrix, second_projector_matrix, output_weight):
    onehot = (residue_chain_index[None, :] == jnp.arange(CHAINS, dtype=jnp.int32)[:, None]).astype(jnp.float32)
    seq_mask = jnp.dot(sequence_row_mask.astype(jnp.float32), onehot, precision=lax.Precision.HIGHEST)
    normalized_input = apply_layer_norm(homolog_embedding, standardize_factor, standardize_shift).astype(jnp.bfloat16)

    def project(weight):
        moved = jnp.einsum('src,ch->srh', normalized_input.astype(jnp.float32), weight.astype(jnp.float32), precision=lax.Precision.HIGHEST)
        return (moved * seq_mask[:, :, None]).astype(jnp.bfloat16)
    left_side = project(first_projector_matrix)
    right_side = project(second_projector_matrix)
    right_wide = right_side.astype(jnp.float32)
    w_cube = output_weight.astype(jnp.float32).reshape(HIDDEN_PER_SIDE, HIDDEN_PER_SIDE, C_Z)
    block_rows = math.gcd(AMINO_COUNT, 64)

    def one_block(row_start):
        left_part = lax.dynamic_slice_in_dim(left_side, row_start, block_rows, 1).astype(jnp.float32)
        mask_part = lax.dynamic_slice_in_dim(seq_mask, row_start, block_rows, 1)
        outer_prod = jnp.einsum('sip,sjq->ipjq', left_part, right_wide, precision=lax.Precision.HIGHEST).astype(jnp.bfloat16)
        projected = jnp.einsum('ipjq,pqz->ijz', outer_prod.astype(jnp.float32), w_cube, precision=lax.Precision.HIGHEST)
        counts = jnp.einsum('si,sj->ij', mask_part, seq_mask, precision=lax.Precision.HIGHEST)
        return (projected / (counts[:, :, None] + 0.001)).astype(jnp.bfloat16)
    starts = jnp.arange(AMINO_COUNT // block_rows, dtype=jnp.int32) * block_rows
    blocks = lax.map(one_block, starts)
    return blocks.reshape(AMINO_COUNT, AMINO_COUNT, C_Z)
```

```python
import functools

import jax
import jax.numpy as jnp
from jax import lax
from jax.experimental import pallas as pl
from jax.experimental.pallas import tpu as pltpu
from jax.sharding import PartitionSpec as P

RING = 4
CORES = 2
SEQS = 4
EMBED = 256
SIDE = 32
PAIR = 128
COLS = 384
ROWS = 48
PLANE = ROWS * CORES
GROUP = SEQS * RING
TOTAL = GROUP * RING * CORES
LANES = 128
RIGHT = (SIDE + 1) * COLS
LEFT = (SIDE + 1) * LANES
MEGA = 2**20
F32 = jnp.float32
BF16 = jnp.bfloat16


def position():
    res = lax.axis_index("res")
    return res // (RING * CORES), (res // CORES) % RING, res % CORES, lax.axis_index("col")


def res_shift(value, dz, dy, dc):
    pairs = []
    for r in range(RING * RING * CORES):
        z, y, c = r // (RING * CORES), (r // CORES) % RING, r % CORES
        to = (((z + dz) % RING) * RING + (y + dy) % RING) * CORES + (c + dc) % CORES
        pairs.append((r, to))
    return lax.ppermute(value, "res", pairs)


def row_owner_shift(value, k):
    pairs = []
    for z in range(RING):
        for y in range(RING):
            for c in range(CORES):
                for x in range(RING):
                    source = ((z * RING + y) * CORES + c) * RING + x
                    target = ((x * RING + y) * CORES + c) * RING + (z + k) % RING
                    pairs.append((source, target))
    return lax.ppermute(value, ("res", "col"), pairs)


def contract_last(a, b):
    return lax.dot_general(a, b, (((1,), (1,)), ((), ())), preferred_element_type=F32)


def project_kernel(emb, weights, chain, chain_parts, gain, shift, first, second, *rest):
    outs, (normed, right, left) = rest[:RING], rest[RING:]
    _, y, _, _ = position()
    first_t = first[...].astype(F32).T.astype(BF16)
    second_t = second[...].astype(F32).T.astype(BF16)
    chains = weights.shape[1]

    def mask_of(row):
        width = row.shape[1]
        ids = lax.broadcasted_iota(jnp.int32, (chains, width), 0)
        onehot = (jnp.broadcast_to(row, (chains, width)) == ids).astype(F32).astype(BF16)
        return jnp.dot(weights[...], onehot, preferred_element_type=F32)

    mask = mask_of(chain[...])
    for s in range(SEQS):
        wide = emb[s].astype(F32)
        shifted = wide - jnp.mean(wide, axis=-1, keepdims=True)
        variance = jnp.mean(shifted * shifted, axis=-1, keepdims=True)
        value = shifted * lax.rsqrt(variance + 1e-05) * gain[...] + shift[...]
        normed[s] = value.astype(BF16)
        right[s] = contract_last(second_t, normed[s]) * mask[s : s + 1]
    for q in range(SIDE):
        part = right[:, q, :].astype(BF16)
        for out in outs:
            out[:, q * COLS : (q + 1) * COLS] = part
    for out in outs:
        out[:, SIDE * COLS : RIGHT] = mask.astype(BF16)
    left[...] = jnp.zeros_like(left)
    for d, out in enumerate(outs):
        to = lax.rem(y + d, RING)
        row_mask = mask_of(chain_parts[pl.ds(to, 1), :])
        start = pl.multiple_of(to * PLANE, 16)
        for s in range(SEQS):
            part = contract_last(first_t, normed[s, pl.ds(start, PLANE), :])
            left[s, 0:SIDE, 0:PLANE] = part * row_mask[s : s + 1]
            left[s, SIDE : SIDE + 1, 0:PLANE] = row_mask[s : s + 1]
        for p in range(SIDE + 1):
            out[:, RIGHT + p * LANES : RIGHT + (p + 1) * LANES] = left[:, p, :].astype(BF16)


def project(emb, weights, chain, gain, shift, first, second):
    return pl.pallas_call(
        project_kernel,
        out_shape=[jax.ShapeDtypeStruct((SEQS, RIGHT + LEFT), BF16)] * RING,
        scratch_shapes=[
            pltpu.VMEM((SEQS, COLS, EMBED), BF16),
            pltpu.VMEM((SEQS, SIDE, COLS), F32),
            pltpu.VMEM((SEQS, SIDE + 8, LANES), F32),
        ],
        compiler_params=pltpu.CompilerParams(vmem_limit_bytes=32 * MEGA),
    )(
        emb,
        weights,
        chain.reshape(1, COLS),
        chain.reshape(RING, PLANE),
        gain.reshape(1, EMBED),
        shift.reshape(1, EMBED),
        first,
        second,
    )


def stack_kernel(*refs):
    parts, (right, left, wide) = refs[:RING], refs[RING:]
    step = 1408
    for at in range(0, RIGHT + LEFT, step):
        for d, part in enumerate(parts):
            wide[d * SEQS : (d + 1) * SEQS, :] = part[:, at : at + step].astype(F32)
        value = wide[...].astype(BF16)
        if at < RIGHT:
            right[:, at : at + step] = value
        else:
            left[:, at - RIGHT : at - RIGHT + step] = value


def stack(parts):
    return pl.pallas_call(
        stack_kernel,
        out_shape=[
            jax.ShapeDtypeStruct((GROUP, RIGHT), BF16),
            jax.ShapeDtypeStruct((GROUP, LEFT), BF16),
        ],
        scratch_shapes=[pltpu.VMEM((GROUP, 1408), F32)],
        compiler_params=pltpu.CompilerParams(vmem_limit_bytes=32 * MEGA),
    )(*parts)


def left_kernel(*refs):
    parts, (out, out_mask, wide, turned) = refs[: RING * CORES], refs[RING * CORES :]
    z, _, core, x = position()
    for c in range(CORES):
        for k in range(RING):
            group = lax.rem(z - x + k + RING, RING)
            start = pl.multiple_of((c * RING + group) * GROUP, GROUP)
            wide[pl.ds(start, GROUP), :] = parts[c * RING + k][...].astype(F32)
    for p in range(SIDE + 1):
        block = wide[:, p * LANES : (p + 1) * LANES].T
        turned[p * PLANE : (p + 1) * PLANE, :] = block[:PLANE]
    base = core * ROWS
    for i in range(ROWS):
        rows = turned[pl.ds(base + i, SIDE, stride=PLANE), :]
        out[i * SIDE : (i + 1) * SIDE, :] = rows.astype(BF16)
    start = pl.multiple_of(SIDE * PLANE + base, 8)
    out_mask[...] = turned[pl.ds(start, ROWS), :].astype(BF16)


def arrange_left(parts):
    return pl.pallas_call(
        left_kernel,
        out_shape=[
            jax.ShapeDtypeStruct((ROWS * SIDE, TOTAL), BF16),
            jax.ShapeDtypeStruct((ROWS, TOTAL), BF16),
        ],
        scratch_shapes=[
            pltpu.VMEM((TOTAL, LEFT), F32),
            pltpu.VMEM(((SIDE + 1) * PLANE, TOTAL), F32),
        ],
        compiler_params=pltpu.CompilerParams(vmem_limit_bytes=32 * MEGA),
    )(*parts)


def pair_kernel(block, left, left_mask, weight, *refs):
    parts, (out, right, outer, scale, sem) = refs[: RING * CORES], refs[RING * CORES :]

    @pl.when(pl.program_id(0) == 0)
    def _():
        copies = [
            pltpu.make_async_copy(part, right.at[pl.ds(k * GROUP, GROUP), :], sem.at[k])
            for k, part in enumerate(parts)
        ]
        for copy in copies:
            copy.start()
        for copy in copies:
            copy.wait()
        counts = jnp.dot(
            left_mask[...], right[:, SIDE * COLS : RIGHT], preferred_element_type=F32
        )
        scale[...] = 1.0 / (counts + 0.001)

    value = left[...]
    for q in range(SIDE):
        part = jnp.dot(
            value, right[:, q * COLS : (q + 1) * COLS], preferred_element_type=F32
        ).astype(BF16)
        for i in range(block):
            outer[i, q * SIDE : (q + 1) * SIDE, :] = part[i * SIDE : (i + 1) * SIDE]
    first = pl.multiple_of(pl.program_id(0) * block, block)
    scales = scale[pl.ds(first, block), :]
    for i in range(block):
        projected = jnp.dot(weight[...], outer[i], preferred_element_type=F32)
        out[i] = (projected * scales[i : i + 1]).T.astype(BF16)


def pair(left, left_mask, weight, parts):
    block = 8
    whole = lambda a: pl.BlockSpec(a.shape, lambda i: (0,) * a.ndim)
    return pl.pallas_call(
        functools.partial(pair_kernel, block),
        grid=(ROWS // block,),
        in_specs=[
            pl.BlockSpec((block * SIDE, TOTAL), lambda i: (i, 0)),
            whole(left_mask),
            whole(weight),
        ]
        + [pl.BlockSpec(memory_space=pl.ANY)] * len(parts),
        out_specs=pl.BlockSpec((block, COLS, PAIR), lambda i: (i, 0, 0)),
        out_shape=jax.ShapeDtypeStruct((ROWS, COLS, PAIR), BF16),
        scratch_shapes=[
            pltpu.VMEM((TOTAL, RIGHT), BF16),
            pltpu.VMEM((block, SIDE * SIDE, COLS), BF16),
            pltpu.VMEM((ROWS, COLS), F32),
            pltpu.SemaphoreType.DMA((RING * CORES,)),
        ],
        compiler_params=pltpu.CompilerParams(vmem_limit_bytes=48 * MEGA),
    )(left, left_mask, weight, *parts)


def local(
    homolog_embedding,
    sequence_row_mask,
    residue_chain_index,
    standardize_factor,
    standardize_shift,
    first_projector_matrix,
    second_projector_matrix,
    output_weight,
):
    weight = output_weight.reshape(SIDE, SIDE, PAIR).transpose(2, 1, 0).reshape(PAIR, SIDE * SIDE)
    own = project(
        homolog_embedding,
        sequence_row_mask,
        residue_chain_index,
        standardize_factor,
        standardize_shift,
        first_projector_matrix,
        second_projector_matrix,
    )
    along_y = [own[0]] + [res_shift(own[d], 0, d, 0) for d in range(1, RING)]
    right, left = stack(along_y)
    right_parts = [right] + [res_shift(right, d, 0, 0) for d in range(1, RING)]
    left_parts = [row_owner_shift(left, k) for k in range(RING)]
    left_parts = left_parts + [res_shift(part, 0, 0, 1) for part in left_parts]
    right_parts = right_parts + [res_shift(part, 0, 0, 1) for part in right_parts]
    left_all, left_mask = arrange_left(left_parts)
    return pair(left_all, left_mask, weight, right_parts)


def solution(mesh):
    in_specs = (P("res", "col", None), P("res", None), P("col"), P(), P(), P(), P(), P())
    out_specs = P("res", "col", None)
    return jax.shard_map(local, mesh=mesh, in_specs=in_specs, out_specs=out_specs, check_vma=False)
```

```python
import functools

import jax
import jax.numpy as jnp
from jax import lax
from jax.experimental import pallas as pl
from jax.experimental.pallas import tpu as pltpu
from jax.sharding import PartitionSpec as P

RING = 4
CORES = 2
SEQS = 4
EMBED = 256
SIDE = 32
PAIR = 128
COLS = 384
ROWS = 48
PLANE = ROWS * CORES
GROUP = SEQS * RING
CHIP = GROUP * CORES
TOTAL = CHIP * RING
LANES = 128
RIGHT = (SIDE + 1) * COLS
MAJOR, MINOR = 64, 32
LEFT = SIDE * PLANE + LANES
MEGA = 2**20
F32 = jnp.float32
BF16 = jnp.bfloat16


def position():
    res = lax.axis_index("res")
    return res // (RING * CORES), (res // CORES) % RING, res % CORES, lax.axis_index("col")


def res_shift(value, dz, dy, dc):
    pairs = []
    for r in range(RING * RING * CORES):
        z, y, c = r // (RING * CORES), (r // CORES) % RING, r % CORES
        to = (((z + dz) % RING) * RING + (y + dy) % RING) * CORES + (c + dc) % CORES
        pairs.append((r, to))
    return lax.ppermute(value, "res", pairs)


def core_swap(value):
    return res_shift(value, 0, 0, 1)


def both_ways(value):
    pairs = []
    for r in range(RING * RING * CORES):
        z, y, c = r // (RING * CORES), (r // CORES) % RING, r % CORES
        pairs.append((r, ((z + (-1 if c else 1)) % RING * RING + y) * CORES + c))
    return lax.ppermute(value, "res", pairs)


def to_row_owner(value, k):
    pairs = []
    for z in range(RING):
        for y in range(RING):
            for c in range(CORES):
                for x in range(RING):
                    source = ((z * RING + y) * CORES + c) * RING + x
                    target = ((x * RING + y) * CORES + c) * RING + (z + k + 2 * c) % RING
                    pairs.append((source, target))
    return lax.ppermute(value, ("res", "col"), pairs)


def contract_last(a, b):
    return lax.dot_general(a, b, (((1,), (1,)), ((), ())), preferred_element_type=F32)


def lanes_of(left, d, first, count, start, width):
    total = None
    lane = lax.broadcasted_iota(jnp.int32, (SEQS, LANES), 1)
    for at in range(count):
        row = left[:, d, first + at, :]
        move = (at * width - start) % LANES
        row = pltpu.roll(row, move, 1) if move else row
        if total is None:
            total = row
        else:
            total = jnp.where(lane >= at * width, row, total)
    return total


def project_kernel(emb, weights, chain, gain, shift, first, second, *rest):
    outs, (both, right, left) = rest[:RING], rest[RING:]
    _, y, _, _ = position()
    chains = weights.shape[1]
    ids = lax.broadcasted_iota(jnp.int32, (chains, COLS), 0)
    row = jnp.broadcast_to(chain[...].reshape(1, COLS), (chains, COLS))
    onehot = (row == ids).astype(F32).astype(BF16)
    mask = jnp.dot(weights[...], onehot, preferred_element_type=F32)
    both[0:SIDE] = first[...]
    both[SIDE:] = second[...]
    turn = lax.rem(RING - y, RING) * PLANE
    for s in range(SEQS):
        wide = emb[s].astype(F32)
        shifted = wide - jnp.mean(wide, axis=-1, keepdims=True)
        variance = jnp.mean(shifted * shifted, axis=-1, keepdims=True)
        value = shifted * lax.rsqrt(variance + 1e-05) * gain[...] + shift[...]
        sides = contract_last(both[...], value.astype(BF16)) * mask[s : s + 1]
        right[s] = sides[SIDE:]
        turned = pltpu.roll(sides[:SIDE], turn, 1)
        row = pltpu.roll(jnp.broadcast_to(mask[s : s + 1], (8, COLS)), turn, 1)
        for d in range(RING):
            left[s, d, 0:SIDE, 0:PLANE] = turned[:, d * PLANE : (d + 1) * PLANE]
            left[s, d, SIDE:, 0:PLANE] = row[:, d * PLANE : (d + 1) * PLANE]
            left[s, d, :, PLANE:] = jnp.zeros((SIDE + 8, LANES - PLANE), F32)
    for q in range(SIDE):
        part = right[:, q, :].astype(BF16)
        for out in outs:
            out[:, q * COLS : (q + 1) * COLS] = part
    for d, out in enumerate(outs):
        out[:, SIDE * COLS : RIGHT] = mask.astype(BF16)
        at = RIGHT
        for p in range(0, SIDE, 2):
            out[:, at : at + LANES] = lanes_of(left, d, p, 2, 0, MAJOR).astype(BF16)
            at += LANES
        for p in range(0, SIDE, 4):
            out[:, at : at + LANES] = lanes_of(left, d, p, 4, MAJOR, MINOR).astype(BF16)
            at += LANES
        out[:, at : at + LANES] = left[:, d, SIDE, :].astype(BF16)


def project(emb, weights, chain, gain, shift, first, second):
    vmem = pl.BlockSpec(memory_space=pltpu.VMEM)
    return pl.pallas_call(
        project_kernel,
        in_specs=[vmem] * 7,
        out_specs=[vmem] * RING,
        out_shape=[jax.ShapeDtypeStruct((SEQS, RIGHT + LEFT), BF16)] * RING,
        scratch_shapes=[
            pltpu.VMEM((2 * SIDE, EMBED), BF16),
            pltpu.VMEM((SEQS, SIDE, COLS), F32),
            pltpu.VMEM((SEQS, RING, SIDE + 8, LANES), F32),
        ],
        compiler_params=pltpu.CompilerParams(vmem_limit_bytes=60 * MEGA),
    )(
        emb,
        weights,
        chain,
        gain.reshape(1, EMBED),
        shift.reshape(1, EMBED),
        first.T,
        second.T,
    )


def stack_kernel(*refs):
    parts, (right, left, own_right, wide) = refs[: RING * CORES], refs[RING * CORES :]
    _, _, core, _ = position()
    step = 2 * COLS
    for at in [*range(0, RIGHT, step), *range(RIGHT, RIGHT + LEFT, step)]:
        out, start = (right, at) if at < RIGHT else (left, at - RIGHT)
        width = min(step, out.shape[1] - start)
        for c in range(CORES):
            base = pl.multiple_of(lax.rem(core + c, CORES) * GROUP, GROUP)
            half = wide.at[pl.ds(base, GROUP)]
            for d in range(RING):
                value = parts[c * RING + d][:, at : at + width].astype(F32)
                half[d * SEQS : (d + 1) * SEQS, :width] = value
            if c == 0 and out is right:
                own_right[:, start : start + width] = half[:, :width].astype(BF16)
        out[:, start : start + width] = wide[:, :width].astype(BF16)


def stack(parts):
    return pl.pallas_call(
        stack_kernel,
        out_shape=[
            jax.ShapeDtypeStruct((CHIP, RIGHT), BF16),
            jax.ShapeDtypeStruct((CHIP, LEFT), BF16),
            jax.ShapeDtypeStruct((GROUP, RIGHT), BF16),
        ],
        scratch_shapes=[pltpu.VMEM((CHIP, 2 * COLS), F32)],
        compiler_params=pltpu.CompilerParams(vmem_limit_bytes=16 * MEGA),
    )(*parts)


def left_kernel(weight, *refs):
    parts, refs = refs[:RING], refs[RING:]
    out, out_mask, out_weight, stacked, turned, wide_weight, sem = refs
    z, _, core, x = position()
    copies = []
    for at, part in enumerate(parts):
        group = lax.rem(z - x + at + 2 * core + RING, RING)
        start = pl.multiple_of(group * CHIP, CHIP)
        copies.append(pltpu.make_async_copy(part, stacked.at[pl.ds(start, CHIP), :], sem.at[at]))
    for copy in copies:
        copy.start()
    wide_weight[...] = weight[...].astype(F32)
    for q in range(0, SIDE, 4):
        rows = [wide_weight[pl.ds(q + at, SIDE, stride=SIDE), :] for at in range(4)]
        out_weight[:, q * SIDE : (q + 4) * SIDE] = jnp.concatenate(rows, 0).T.astype(BF16)
    for copy in copies:
        copy.wait()

    def block_at(at):
        return stacked[:, at : at + LANES].astype(F32).T

    at = 0
    for p in range(0, SIDE, 2):
        block = block_at(at)
        at += LANES
        for k in range(2):
            turned[(p + k) * PLANE : (p + k) * PLANE + MAJOR, :] = block[k * MAJOR : (k + 1) * MAJOR]
    for p in range(0, SIDE, 4):
        block = block_at(at)
        at += LANES
        for k in range(4):
            row = (p + k) * PLANE + MAJOR
            turned[row : row + MINOR, :] = block[k * MINOR : (k + 1) * MINOR]
    turned[SIDE * PLANE :, :] = block_at(at)[:PLANE]
    base = core * ROWS
    for i in range(ROWS):
        rows = turned[pl.ds(base + i, SIDE, stride=PLANE), :]
        out[i * SIDE : (i + 1) * SIDE, :] = rows.astype(BF16)
    start = pl.multiple_of(SIDE * PLANE + base, 8)
    out_mask[...] = turned[pl.ds(start, ROWS), :].astype(BF16)


def arrange_left(weight, parts):
    vmem = pl.BlockSpec(memory_space=pltpu.VMEM)
    return pl.pallas_call(
        left_kernel,
        in_specs=[vmem] + [pl.BlockSpec(memory_space=pl.ANY)] * len(parts),
        out_specs=[vmem] * 3,
        out_shape=[
            jax.ShapeDtypeStruct((ROWS * SIDE, TOTAL), BF16),
            jax.ShapeDtypeStruct((ROWS, TOTAL), BF16),
            jax.ShapeDtypeStruct((PAIR, SIDE * SIDE), BF16),
        ],
        scratch_shapes=[
            pltpu.VMEM((TOTAL, LEFT), BF16),
            pltpu.VMEM(((SIDE + 1) * PLANE, TOTAL), F32),
            pltpu.VMEM((SIDE * SIDE, PAIR), F32),
            pltpu.SemaphoreType.DMA((RING,)),
        ],
        compiler_params=pltpu.CompilerParams(vmem_limit_bytes=32 * MEGA),
    )(weight, *parts)


def pair_kernel(block, left, left_mask, weight, *refs):
    parts, (out, right, outer, scale, sem) = refs[: RING + 1], refs[RING + 1 :]
    _, _, core, _ = position()

    @pl.when(pl.program_id(0) == 0)
    def _():
        starts = [0, (1 + 2 * core) * CHIP, (3 - 2 * core) * CHIP]
        starts += [2 * CHIP + core * GROUP, 2 * CHIP + (1 - core) * GROUP]
        copies = []
        for k, part in enumerate(parts):
            rows = pl.ds(pl.multiple_of(starts[k], GROUP), part.shape[0])
            copies.append(pltpu.make_async_copy(part, right.at[rows, :], sem.at[k]))
        for copy in copies:
            copy.start()
        for copy in copies:
            copy.wait()
        counts = jnp.dot(
            left_mask[...], right[:, SIDE * COLS : (SIDE + 1) * COLS], preferred_element_type=F32
        )
        scale[...] = 1.0 / (counts + 0.001)

    value = left[...]
    for q in range(SIDE):
        part = jnp.dot(
            value, right[:, q * COLS : (q + 1) * COLS], preferred_element_type=F32
        ).astype(BF16)
        for i in range(block):
            outer[i, q * SIDE : (q + 1) * SIDE, :] = part[i * SIDE : (i + 1) * SIDE]
    first = pl.multiple_of(pl.program_id(0) * block, block)
    scales = scale[pl.ds(first, block), :]
    for i in range(block):
        projected = jnp.dot(weight[...], outer[i], preferred_element_type=F32)
        out[i] = (projected * scales[i : i + 1]).T.astype(BF16)


def pair(left, left_mask, weight, parts):
    block = 8
    whole = lambda a: pl.BlockSpec(a.shape, lambda i: (0,) * a.ndim)
    return pl.pallas_call(
        functools.partial(pair_kernel, block),
        grid=(ROWS // block,),
        in_specs=[
            pl.BlockSpec((block * SIDE, TOTAL), lambda i: (i, 0)),
            whole(left_mask),
            whole(weight),
        ]
        + [pl.BlockSpec(memory_space=pl.ANY)] * len(parts),
        out_specs=pl.BlockSpec((block, COLS, PAIR), lambda i: (i, 0, 0)),
        out_shape=jax.ShapeDtypeStruct((ROWS, COLS, PAIR), BF16),
        scratch_shapes=[
            pltpu.VMEM((TOTAL, RIGHT), BF16),
            pltpu.VMEM((block, SIDE * SIDE, COLS), BF16),
            pltpu.VMEM((ROWS, COLS), F32),
            pltpu.SemaphoreType.DMA((RING + 1,)),
        ],
        compiler_params=pltpu.CompilerParams(vmem_limit_bytes=48 * MEGA),
    )(left, left_mask, weight, *parts)


def local(
    homolog_embedding,
    sequence_row_mask,
    residue_chain_index,
    standardize_factor,
    standardize_shift,
    first_projector_matrix,
    second_projector_matrix,
    output_weight,
):
    own = project(
        homolog_embedding,
        sequence_row_mask,
        residue_chain_index,
        standardize_factor,
        standardize_shift,
        first_projector_matrix,
        second_projector_matrix,
    )
    along_y = [own[0]] + [res_shift(own[d], 0, d, 0) for d in range(1, RING)]
    right, left, own_right = stack(along_y + [core_swap(part) for part in along_y])
    left_parts = [to_row_owner(left, k) for k in range(2)]
    near, far = both_ways(right), res_shift(own_right, 2, 0, 0)
    prepared = arrange_left(output_weight, left_parts + [core_swap(part) for part in left_parts])
    prepared, near, far = lax.optimization_barrier((prepared, near, far))
    return pair(*prepared, [right, near, core_swap(near), far, core_swap(far)])


def solution(mesh):
    in_specs = (P("res", "col", None), P("res", None), P("col"), P(), P(), P(), P(), P())
    out_specs = P("res", "col", None)
    return jax.shard_map(local, mesh=mesh, in_specs=in_specs, out_specs=out_specs, check_vma=False)
```

```python
import functools

import jax
import jax.numpy as jnp
from jax import lax
from jax.experimental import pallas as pl
from jax.experimental.pallas import tpu as pltpu
from jax.sharding import PartitionSpec as P

RING = 4
CORES = 2
SEQS = 4
EMBED = 256
SIDE = 32
PAIR = 128
COLS = 384
ROWS = 48
PLANE = ROWS * CORES
GROUP = SEQS * RING
CHIP = GROUP * CORES
TOTAL = CHIP * RING
LANES = 128
RIGHT = (SIDE + 1) * COLS
MAJOR, MINOR = 64, 32
LEFT = SIDE * PLANE + LANES
MEGA = 2**20
F32 = jnp.float32
BF16 = jnp.bfloat16


def position():
    res = lax.axis_index("res")
    return res // (RING * CORES), (res // CORES) % RING, res % CORES, lax.axis_index("col")


def res_shift(value, dz, dy, dc):
    pairs = []
    for r in range(RING * RING * CORES):
        z, y, c = r // (RING * CORES), (r // CORES) % RING, r % CORES
        to = (((z + dz) % RING) * RING + (y + dy) % RING) * CORES + (c + dc) % CORES
        pairs.append((r, to))
    return lax.ppermute(value, "res", pairs)


def core_swap(value):
    return res_shift(value, 0, 0, 1)


def both_ways(value, dz, dy):
    pairs = []
    for r in range(RING * RING * CORES):
        z, y, c = r // (RING * CORES), (r // CORES) % RING, r % CORES
        way = -1 if c else 1
        z, y = (z + way * dz) % RING, (y + way * dy) % RING
        pairs.append((r, (z * RING + y) * CORES + c))
    return lax.ppermute(value, "res", pairs)


def to_row_owner(value, k):
    pairs = []
    for z in range(RING):
        for y in range(RING):
            for c in range(CORES):
                for x in range(RING):
                    source = ((z * RING + y) * CORES + c) * RING + x
                    target = ((x * RING + y) * CORES + c) * RING + (z + k + 2 * c) % RING
                    pairs.append((source, target))
    return lax.ppermute(value, ("res", "col"), pairs)


def contract_last(a, b):
    return lax.dot_general(a, b, (((1,), (1,)), ((), ())), preferred_element_type=F32)


def side_by_side(value, count, start, width):
    rows = value.shape[0] // count
    lane = lax.broadcasted_iota(jnp.int32, (rows, LANES), 1)
    total = None
    for at in range(count):
        part = value[at * rows : (at + 1) * rows]
        move = (at * width - start) % LANES
        part = pltpu.roll(part, move, 1) if move else part
        total = part if total is None else jnp.where(lane >= at * width, part, total)
    return total


def project_kernel(*refs):
    arguments, outs = refs[:7], refs[7 : 8 + RING]
    emb, weights, chain, gain, shift, first, second = arguments
    both, right, left = refs[8 + RING :]
    _, y, _, _ = position()
    chains = weights.shape[1]
    ids = lax.broadcasted_iota(jnp.int32, (chains, COLS), 0)
    row = jnp.broadcast_to(chain[...].reshape(1, COLS), (chains, COLS))
    onehot = (row == ids).astype(F32).astype(BF16)
    mask = jnp.dot(weights[...], onehot, preferred_element_type=F32)
    both[0:SIDE] = first[...]
    both[SIDE:] = second[...]
    turn = lax.rem(RING - y, RING) * PLANE
    for s in range(SEQS):
        wide = emb[s].astype(F32)
        shifted = wide - jnp.mean(wide, axis=-1, keepdims=True)
        variance = jnp.mean(shifted * shifted, axis=-1, keepdims=True)
        value = shifted * lax.rsqrt(variance + 1e-05) * gain[...].reshape(1, EMBED)
        value = (value + shift[...].reshape(1, EMBED)).astype(BF16)
        sides = contract_last(both[...], value) * mask[s : s + 1]
        right[s] = sides[SIDE:]
        turned = pltpu.roll(sides[:SIDE], turn, 1)
        row = pltpu.roll(jnp.broadcast_to(mask[s : s + 1], (8, COLS)), turn, 1)
        fill = jnp.zeros((SIDE, LANES - PLANE), F32)
        for d in range(RING):
            part = jnp.concatenate([turned[:, d * PLANE : (d + 1) * PLANE], fill], 1)
            left[s, d, 0 : SIDE // 2] = side_by_side(part, 2, 0, MAJOR)
            left[s, d, SIDE // 2 : 3 * SIDE // 4] = side_by_side(part, 4, MAJOR, MINOR)
            part = jnp.concatenate([row[:, d * PLANE : (d + 1) * PLANE], fill[:8]], 1)
            left[s, d, 3 * SIDE // 4 :] = part
    for q in range(SIDE):
        part = right[:, q, :].astype(BF16)
        for out in outs:
            out[:, q * COLS : (q + 1) * COLS] = part
    for out in outs:
        out[:, SIDE * COLS : RIGHT] = mask.astype(BF16)
    for d, out in enumerate(outs[:RING]):
        for at in range(LEFT // LANES):
            to = RIGHT + at * LANES
            out[:, to : to + LANES] = left[:, d, at, :].astype(BF16)


def project(emb, weights, chain, gain, shift, first, second):
    arguments = (emb, weights, chain, gain, shift, first.T, second.T)
    return pl.pallas_call(
        project_kernel,
        in_specs=[pl.BlockSpec(memory_space=pltpu.VMEM)] * len(arguments),
        out_specs=[pl.BlockSpec(memory_space=pltpu.VMEM)] * (RING + 1),
        out_shape=[jax.ShapeDtypeStruct((SEQS, RIGHT + LEFT), BF16)] * RING
        + [jax.ShapeDtypeStruct((SEQS, RIGHT), BF16)],
        scratch_shapes=[
            pltpu.VMEM((2 * SIDE, EMBED), BF16),
            pltpu.VMEM((SEQS, SIDE, COLS), F32),
            pltpu.VMEM((SEQS, RING, LEFT // LANES + 7, LANES), F32),
        ],
        compiler_params=pltpu.CompilerParams(vmem_limit_bytes=60 * MEGA),
    )(*arguments)


def weight_kernel(weight_hbm, out, weight, wide, sem):
    copy = pltpu.make_async_copy(weight_hbm, weight, sem)
    copy.start()
    copy.wait()
    wide[...] = weight[...].astype(F32)
    for q in range(0, SIDE, 4):
        rows = [wide[pl.ds(q + at, SIDE, stride=SIDE), :] for at in range(4)]
        out[:, q * SIDE : (q + 4) * SIDE] = jnp.concatenate(rows, 0).T.astype(BF16)


def arrange_weight(weight):
    return pl.pallas_call(
        weight_kernel,
        in_specs=[pl.BlockSpec(memory_space=pl.ANY)],
        out_specs=pl.BlockSpec(memory_space=pltpu.VMEM),
        out_shape=jax.ShapeDtypeStruct((PAIR, SIDE * SIDE), BF16),
        scratch_shapes=[
            pltpu.VMEM((SIDE * SIDE, PAIR), BF16),
            pltpu.VMEM((SIDE * SIDE, PAIR), F32),
            pltpu.SemaphoreType.DMA,
        ],
        compiler_params=pltpu.CompilerParams(vmem_limit_bytes=16 * MEGA),
    )(weight)


def chunks(width):
    return [(at, min(2 * COLS, width - at)) for at in range(0, width, 2 * COLS)]


def by_core(core, own, other):
    return jnp.where(core == 0, own, other), jnp.where(core == 0, other, own)


def stack_kernel(*refs):
    parts, (far, far_other, right, left, far_chip, wide) = refs[: RING * CORES], refs[RING * CORES :]
    _, _, core, _ = position()
    for out, base in ((right, 0), (left, RIGHT)):
        for at, width in chunks(out.shape[1]):
            lanes = slice(base + at, base + at + width)
            for c in range(CORES):
                start = pl.multiple_of(lax.rem(core + c, CORES) * GROUP, GROUP)
                half = wide.at[pl.ds(start, GROUP)]
                for d in range(RING):
                    half[d * SEQS : (d + 1) * SEQS, :width] = parts[c * RING + d][:, lanes].astype(F32)
            out[:, at : at + width] = wide[:, :width].astype(BF16)
    for at, width in chunks(RIGHT):
        lanes = slice(at, at + width)
        values = by_core(core, far[:, lanes].astype(F32), far_other[:, lanes].astype(F32))
        for c in range(CORES):
            wide[c * SEQS : (c + 1) * SEQS, :width] = values[c]
        far_chip[:, lanes] = wide[: CORES * SEQS, :width].astype(BF16)


def stack(parts, far, far_other):
    return pl.pallas_call(
        stack_kernel,
        out_shape=[
            jax.ShapeDtypeStruct((CHIP, RIGHT), BF16),
            jax.ShapeDtypeStruct((CHIP, LEFT), BF16),
            jax.ShapeDtypeStruct((CORES * SEQS, RIGHT), BF16),
        ],
        scratch_shapes=[pltpu.VMEM((CHIP, 2 * COLS), F32)],
        compiler_params=pltpu.CompilerParams(vmem_limit_bytes=16 * MEGA),
    )(*parts, far, far_other)


def far_kernel(own, near, near_other, far, far_other, out, wide):
    _, _, core, _ = position()
    for at, width in chunks(RIGHT):
        lanes = slice(at, at + width)
        below, above = by_core(core, near[:, lanes].astype(F32), near_other[:, lanes].astype(F32))
        opposite = by_core(core, far[:, lanes].astype(F32), far_other[:, lanes].astype(F32))
        here = own[:, lanes].astype(F32)
        for c in range(CORES):
            rows = slice(c * SEQS, (c + 1) * SEQS)
            for d, value in enumerate((here[rows], below[rows], opposite[c], above[rows])):
                start = c * GROUP + d * SEQS
                wide[start : start + SEQS, :width] = value
        out[:, lanes] = wide[:, :width].astype(BF16)


def stack_far(*parts):
    return pl.pallas_call(
        far_kernel,
        out_shape=jax.ShapeDtypeStruct((CHIP, RIGHT), BF16),
        scratch_shapes=[pltpu.VMEM((CHIP, 2 * COLS), F32)],
        compiler_params=pltpu.CompilerParams(vmem_limit_bytes=16 * MEGA),
    )(*parts)


def left_kernel(*refs):
    parts, (out, out_mask, stacked, turned, sem) = refs[:RING], refs[RING:]
    z, _, core, x = position()
    copies = []
    for at, part in enumerate(parts):
        group = lax.rem(z - x + at + 2 * core + RING, RING)
        start = pl.multiple_of(group * CHIP, CHIP)
        copies.append(pltpu.make_async_copy(part, stacked.at[pl.ds(start, CHIP), :], sem.at[at]))
    for copy in copies:
        copy.start()
    for copy in copies:
        copy.wait()

    def block_at(at):
        return stacked[:, at * LANES : (at + 1) * LANES].astype(F32).T

    for p in range(SIDE // 2):
        block = block_at(p)
        for k in range(2):
            row = (p + k * SIDE // 2) * PLANE
            turned[row : row + MAJOR, :] = block[k * MAJOR : (k + 1) * MAJOR]
    for p in range(SIDE // 4):
        block = block_at(SIDE // 2 + p)
        for k in range(4):
            row = (p + k * SIDE // 4) * PLANE + MAJOR
            turned[row : row + MINOR, :] = block[k * MINOR : (k + 1) * MINOR]
    turned[SIDE * PLANE :, :] = block_at(3 * SIDE // 4)[:PLANE]
    base = core * ROWS
    for i in range(ROWS):
        rows = turned[pl.ds(base + i, SIDE, stride=PLANE), :]
        out[i * SIDE : (i + 1) * SIDE, :] = rows.astype(BF16)
    start = pl.multiple_of(SIDE * PLANE + base, 8)
    out_mask[...] = turned[pl.ds(start, ROWS), :].astype(BF16)


def arrange_left(parts):
    return pl.pallas_call(
        left_kernel,
        in_specs=[pl.BlockSpec(memory_space=pl.ANY)] * len(parts),
        out_specs=[pl.BlockSpec(memory_space=pltpu.VMEM)] * 2,
        out_shape=[
            jax.ShapeDtypeStruct((ROWS * SIDE, TOTAL), BF16),
            jax.ShapeDtypeStruct((ROWS, TOTAL), BF16),
        ],
        scratch_shapes=[
            pltpu.VMEM((TOTAL, LEFT), BF16),
            pltpu.VMEM(((SIDE + 1) * PLANE, TOTAL), F32),
            pltpu.SemaphoreType.DMA((RING,)),
        ],
        compiler_params=pltpu.CompilerParams(vmem_limit_bytes=16 * MEGA),
    )(*parts)


def pair_kernel(block, beside, left, left_mask, weight, *refs):
    parts, (out, right, outer, scale, sem) = refs[:RING], refs[RING:]
    _, _, core, _ = position()

    @pl.when(pl.program_id(0) == 0)
    def _():
        copies = []
        for k, slot in enumerate((0, 1 + 2 * core, 3 - 2 * core, 2)):
            rows = pl.ds(pl.multiple_of(slot * CHIP, CHIP), CHIP)
            copies.append(pltpu.make_async_copy(parts[k], right.at[rows, :], sem.at[k]))
        for copy in copies:
            copy.start()
        for copy in copies:
            copy.wait()
        counts = jnp.dot(left_mask[...], right[:, SIDE * COLS :], preferred_element_type=F32)
        scale[...] = 1.0 / (counts + 0.001)

    value = left[...]
    for q in range(SIDE):
        part = jnp.dot(
            value, right[:, q * COLS : (q + 1) * COLS], preferred_element_type=F32
        ).astype(BF16)
        for i in range(block):
            at = i % beside * COLS
            outer[i // beside, q * SIDE : (q + 1) * SIDE, at : at + COLS] = part[
                i * SIDE : (i + 1) * SIDE
            ]
    first = pl.multiple_of(pl.program_id(0) * block, block)
    scales = scale[pl.ds(first, block), :]
    for i in range(0, block, beside):
        projected = jnp.dot(weight[...], outer[i // beside], preferred_element_type=F32)
        for k in range(beside):
            value = projected[:, k * COLS : (k + 1) * COLS] * scales[i + k : i + k + 1]
            out[i + k] = value.T.astype(BF16)


def pair(left, left_mask, weight, parts):
    block, beside = 8, 2
    whole = lambda a: pl.BlockSpec(a.shape, lambda i: (0,) * a.ndim)
    return pl.pallas_call(
        functools.partial(pair_kernel, block, beside),
        grid=(ROWS // block,),
        in_specs=[
            pl.BlockSpec((block * SIDE, TOTAL), lambda i: (i, 0)),
            whole(left_mask),
            whole(weight),
        ]
        + [pl.BlockSpec(memory_space=pl.ANY)] * len(parts),
        out_specs=pl.BlockSpec((block, COLS, PAIR), lambda i: (i, 0, 0)),
        out_shape=jax.ShapeDtypeStruct((ROWS, COLS, PAIR), BF16),
        scratch_shapes=[
            pltpu.VMEM((TOTAL, RIGHT), BF16),
            pltpu.VMEM((block // beside, SIDE * SIDE, beside * COLS), BF16),
            pltpu.VMEM((ROWS, COLS), F32),
            pltpu.SemaphoreType.DMA((RING,)),
        ],
        compiler_params=pltpu.CompilerParams(vmem_limit_bytes=40 * MEGA),
    )(left, left_mask, weight, *parts)


def local(
    homolog_embedding,
    sequence_row_mask,
    residue_chain_index,
    standardize_factor,
    standardize_shift,
    first_projector_matrix,
    second_projector_matrix,
    output_weight,
):
    own = project(
        homolog_embedding,
        sequence_row_mask,
        residue_chain_index,
        standardize_factor,
        standardize_shift,
        first_projector_matrix,
        second_projector_matrix,
    )
    along_y = [own[0]] + [res_shift(own[d], 0, d, 0) for d in range(1, RING)]
    far = res_shift(own[RING], 2, 0, 0)
    weight = arrange_weight(output_weight)
    along_y[2], weight = lax.optimization_barrier((along_y[2], weight))
    right, left, far_chip = stack(along_y + [core_swap(part) for part in along_y], far, core_swap(far))
    near = both_ways(right, 1, 0)
    left_parts = [to_row_owner(left, k) for k in range(2)]
    far_parts = [both_ways(far_chip, 0, 1), res_shift(far, 0, 2, 0)]
    left_parts, far_parts = lax.optimization_barrier((left_parts, far_parts))
    sides = arrange_left(left_parts + [core_swap(part) for part in left_parts])
    far_right = stack_far(
        far_chip, far_parts[0], core_swap(far_parts[0]), far_parts[1], core_swap(far_parts[1])
    )
    sides, far_right, near = lax.optimization_barrier((sides, far_right, near))
    return pair(*sides, weight, [right, near, core_swap(near), far_right])


def solution(mesh):
    in_specs = (P("res", "col", None), P("res", None), P("col"), P(), P(), P(), P(), P())
    out_specs = P("res", "col", None)
    return jax.shard_map(local, mesh=mesh, in_specs=in_specs, out_specs=out_specs, check_vma=False)
```

```python
import functools

import jax
import jax.numpy as jnp
from jax import lax
from jax.experimental import pallas as pl
from jax.experimental.pallas import tpu as pltpu
from jax.sharding import PartitionSpec as P

RING = 4
CORES = 2
SEQS = 4
EMBED = 256
SIDE = 32
PAIR = 128
COLS = 384
ROWS = 48
PLANE = ROWS * CORES
GROUP = SEQS * RING
CHIP = GROUP * CORES
TOTAL = CHIP * RING
LANES = 128
RIGHT = (SIDE + 1) * COLS
MAJOR, MINOR = 64, 32
LEFT = SIDE * PLANE + LANES
MEGA = 2**20
F32 = jnp.float32
BF16 = jnp.bfloat16


def position():
    res = lax.axis_index("res")
    return res // (RING * CORES), (res // CORES) % RING, res % CORES, lax.axis_index("col")


def res_shift(value, dz, dy, dc):
    pairs = []
    for r in range(RING * RING * CORES):
        z, y, c = r // (RING * CORES), (r // CORES) % RING, r % CORES
        to = (((z + dz) % RING) * RING + (y + dy) % RING) * CORES + (c + dc) % CORES
        pairs.append((r, to))
    return lax.ppermute(value, "res", pairs)


def core_swap(value):
    return res_shift(value, 0, 0, 1)


def both_ways(value, dz, dy):
    pairs = []
    for r in range(RING * RING * CORES):
        z, y, c = r // (RING * CORES), (r // CORES) % RING, r % CORES
        way = -1 if c else 1
        z, y = (z + way * dz) % RING, (y + way * dy) % RING
        pairs.append((r, (z * RING + y) * CORES + c))
    return lax.ppermute(value, "res", pairs)


def to_row_owner(value, k):
    pairs = []
    for z in range(RING):
        for y in range(RING):
            for c in range(CORES):
                for x in range(RING):
                    source = ((z * RING + y) * CORES + c) * RING + x
                    target = ((x * RING + y) * CORES + c) * RING + (z + k + 2 * c) % RING
                    pairs.append((source, target))
    return lax.ppermute(value, ("res", "col"), pairs)


def contract_last(a, b):
    return lax.dot_general(a, b, (((1,), (1,)), ((), ())), preferred_element_type=F32)


def side_by_side(value, count, start, width):
    rows = value.shape[0] // count
    lane = lax.broadcasted_iota(jnp.int32, (rows, LANES), 1)
    total = None
    for at in range(count):
        part = value[at * rows : (at + 1) * rows]
        move = (at * width - start) % LANES
        part = pltpu.roll(part, move, 1) if move else part
        total = part if total is None else jnp.where(lane >= at * width, part, total)
    return total


def project_kernel(*refs):
    arguments, outs = refs[:7], refs[7 : 8 + RING]
    emb, weights, chain, gain, shift, first, second = arguments
    both, right, left = refs[8 + RING :]
    _, y, _, _ = position()
    chains = weights.shape[1]
    ids = lax.broadcasted_iota(jnp.int32, (chains, COLS), 0)
    row = jnp.broadcast_to(chain[...].reshape(1, COLS), (chains, COLS))
    onehot = (row == ids).astype(F32).astype(BF16)
    mask = jnp.dot(weights[...], onehot, preferred_element_type=F32)
    both[0:SIDE] = first[...]
    both[SIDE:] = second[...]
    turn = lax.rem(RING - y, RING) * PLANE
    for s in range(SEQS):
        wide = emb[s].astype(F32)
        shifted = wide - jnp.mean(wide, axis=-1, keepdims=True)
        variance = jnp.mean(shifted * shifted, axis=-1, keepdims=True)
        value = shifted * lax.rsqrt(variance + 1e-05) * gain[...].reshape(1, EMBED)
        value = (value + shift[...].reshape(1, EMBED)).astype(BF16)
        sides = contract_last(both[...], value) * mask[s : s + 1]
        right[s] = sides[SIDE:]
        turned = pltpu.roll(sides[:SIDE], turn, 1)
        row = pltpu.roll(jnp.broadcast_to(mask[s : s + 1], (8, COLS)), turn, 1)
        fill = jnp.zeros((SIDE, LANES - PLANE), F32)
        for d in range(RING):
            part = jnp.concatenate([turned[:, d * PLANE : (d + 1) * PLANE], fill], 1)
            left[s, d, 0 : SIDE // 2] = side_by_side(part, 2, 0, MAJOR)
            left[s, d, SIDE // 2 : 3 * SIDE // 4] = side_by_side(part, 4, MAJOR, MINOR)
            part = jnp.concatenate([row[:, d * PLANE : (d + 1) * PLANE], fill[:8]], 1)
            left[s, d, 3 * SIDE // 4 :] = part
    for q in range(SIDE):
        part = right[:, q, :].astype(BF16)
        for out in outs:
            out[:, q * COLS : (q + 1) * COLS] = part
    for out in outs:
        out[:, SIDE * COLS : RIGHT] = mask.astype(BF16)
    for d, out in enumerate(outs[:RING]):
        for at in range(LEFT // LANES):
            to = RIGHT + at * LANES
            out[:, to : to + LANES] = left[:, d, at, :].astype(BF16)


def project(emb, weights, chain, gain, shift, first, second):
    arguments = (emb, weights, chain, gain, shift, first.T, second.T)
    return pl.pallas_call(
        project_kernel,
        in_specs=[pl.BlockSpec(memory_space=pltpu.VMEM)] * len(arguments),
        out_specs=[pl.BlockSpec(memory_space=pltpu.VMEM)] * (RING + 1),
        out_shape=[pltpu.VMEM((SEQS, RIGHT + LEFT), BF16)] * RING
        + [pltpu.VMEM((SEQS, RIGHT), BF16)],
        scratch_shapes=[
            pltpu.VMEM((2 * SIDE, EMBED), BF16),
            pltpu.VMEM((SEQS, SIDE, COLS), F32),
            pltpu.VMEM((SEQS, RING, LEFT // LANES + 7, LANES), F32),
        ],
        compiler_params=pltpu.CompilerParams(vmem_limit_bytes=60 * MEGA),
    )(*arguments)


def weight_kernel(weight_hbm, out, weight, wide, sem):
    copy = pltpu.make_async_copy(weight_hbm, weight, sem)
    copy.start()
    copy.wait()
    wide[...] = weight[...].astype(F32)
    for q in range(0, SIDE, 4):
        rows = [wide[pl.ds(q + at, SIDE, stride=SIDE), :] for at in range(4)]
        out[:, q * SIDE : (q + 4) * SIDE] = jnp.concatenate(rows, 0).T.astype(BF16)


def arrange_weight(weight):
    return pl.pallas_call(
        weight_kernel,
        in_specs=[pl.BlockSpec(memory_space=pl.ANY)],
        out_specs=pl.BlockSpec(memory_space=pltpu.VMEM),
        out_shape=jax.ShapeDtypeStruct((PAIR, SIDE * SIDE), BF16),
        scratch_shapes=[
            pltpu.VMEM((SIDE * SIDE, PAIR), BF16),
            pltpu.VMEM((SIDE * SIDE, PAIR), F32),
            pltpu.SemaphoreType.DMA,
        ],
        compiler_params=pltpu.CompilerParams(vmem_limit_bytes=16 * MEGA),
    )(weight)


def chunks(width):
    return [(at, min(2 * COLS, width - at)) for at in range(0, width, 2 * COLS)]


def by_core(core, own, other):
    return jnp.where(core == 0, own, other), jnp.where(core == 0, other, own)


def stack_kernel(*refs):
    parts, (far, far_other, right, left, far_chip, wide) = refs[: RING * CORES], refs[RING * CORES :]
    _, _, core, _ = position()
    for out, base in ((right, 0), (left, RIGHT)):
        for at, width in chunks(out.shape[1]):
            lanes = slice(base + at, base + at + width)
            for c in range(CORES):
                start = pl.multiple_of(lax.rem(core + c, CORES) * GROUP, GROUP)
                half = wide.at[pl.ds(start, GROUP)]
                for d in range(RING):
                    half[d * SEQS : (d + 1) * SEQS, :width] = parts[c * RING + d][:, lanes].astype(F32)
            out[:, at : at + width] = wide[:, :width].astype(BF16)
    for at, width in chunks(RIGHT):
        lanes = slice(at, at + width)
        values = by_core(core, far[:, lanes].astype(F32), far_other[:, lanes].astype(F32))
        for c in range(CORES):
            wide[c * SEQS : (c + 1) * SEQS, :width] = values[c]
        far_chip[:, lanes] = wide[: CORES * SEQS, :width].astype(BF16)


def stack(parts, far, far_other):
    return pl.pallas_call(
        stack_kernel,
        out_shape=[
            jax.ShapeDtypeStruct((CHIP, RIGHT), BF16),
            jax.ShapeDtypeStruct((CHIP, LEFT), BF16),
            jax.ShapeDtypeStruct((CORES * SEQS, RIGHT), BF16),
        ],
        scratch_shapes=[pltpu.VMEM((CHIP, 2 * COLS), F32)],
        compiler_params=pltpu.CompilerParams(vmem_limit_bytes=16 * MEGA),
    )(*parts, far, far_other)


def far_kernel(own, near, near_other, far, far_other, out, wide):
    _, _, core, _ = position()
    for at, width in chunks(RIGHT):
        lanes = slice(at, at + width)
        below, above = by_core(core, near[:, lanes].astype(F32), near_other[:, lanes].astype(F32))
        opposite = by_core(core, far[:, lanes].astype(F32), far_other[:, lanes].astype(F32))
        here = own[:, lanes].astype(F32)
        for c in range(CORES):
            rows = slice(c * SEQS, (c + 1) * SEQS)
            for d, value in enumerate((here[rows], below[rows], opposite[c], above[rows])):
                start = c * GROUP + d * SEQS
                wide[start : start + SEQS, :width] = value
        out[:, lanes] = wide[:, :width].astype(BF16)


def stack_far(*parts):
    return pl.pallas_call(
        far_kernel,
        out_shape=jax.ShapeDtypeStruct((CHIP, RIGHT), BF16),
        scratch_shapes=[pltpu.VMEM((CHIP, 2 * COLS), F32)],
        compiler_params=pltpu.CompilerParams(vmem_limit_bytes=16 * MEGA),
    )(*parts)


def left_kernel(*refs):
    parts, (out, out_mask, stacked, turned, sem) = refs[:RING], refs[RING:]
    z, _, core, x = position()
    copies = []
    for at, part in enumerate(parts):
        group = lax.rem(z - x + at + 2 * core + RING, RING)
        start = pl.multiple_of(group * CHIP, CHIP)
        copies.append(pltpu.make_async_copy(part, stacked.at[pl.ds(start, CHIP), :], sem.at[at]))
    for copy in copies:
        copy.start()
    for copy in copies:
        copy.wait()

    def block_at(at):
        return stacked[:, at * LANES : (at + 1) * LANES].astype(F32).T

    for p in range(SIDE // 2):
        block = block_at(p)
        for k in range(2):
            row = (p + k * SIDE // 2) * PLANE
            turned[row : row + MAJOR, :] = block[k * MAJOR : (k + 1) * MAJOR]
    for p in range(SIDE // 4):
        block = block_at(SIDE // 2 + p)
        for k in range(4):
            row = (p + k * SIDE // 4) * PLANE + MAJOR
            turned[row : row + MINOR, :] = block[k * MINOR : (k + 1) * MINOR]
    turned[SIDE * PLANE :, :] = block_at(3 * SIDE // 4)[:PLANE]
    base = core * ROWS
    for i in range(ROWS):
        rows = turned[pl.ds(base + i, SIDE, stride=PLANE), :]
        out[i * SIDE : (i + 1) * SIDE, :] = rows.astype(BF16)
    start = pl.multiple_of(SIDE * PLANE + base, 8)
    out_mask[...] = turned[pl.ds(start, ROWS), :].astype(BF16)


def arrange_left(parts):
    return pl.pallas_call(
        left_kernel,
        in_specs=[pl.BlockSpec(memory_space=pl.ANY)] * len(parts),
        out_specs=[pl.BlockSpec(memory_space=pltpu.VMEM)] * 2,
        out_shape=[
            jax.ShapeDtypeStruct((ROWS * SIDE, TOTAL), BF16),
            jax.ShapeDtypeStruct((ROWS, TOTAL), BF16),
        ],
        scratch_shapes=[
            pltpu.VMEM((TOTAL, LEFT), BF16),
            pltpu.VMEM(((SIDE + 1) * PLANE, TOTAL), F32),
            pltpu.SemaphoreType.DMA((RING,)),
        ],
        compiler_params=pltpu.CompilerParams(vmem_limit_bytes=16 * MEGA),
    )(*parts)


def pair_kernel(block, beside, left, left_mask, weight, *refs):
    parts, (out, right, outer, scale, sem) = refs[:RING], refs[RING:]
    _, _, core, _ = position()

    @pl.when(pl.program_id(0) == 0)
    def _():
        copies = []
        for k, slot in enumerate((0, 1 + 2 * core, 3 - 2 * core, 2)):
            rows = pl.ds(pl.multiple_of(slot * CHIP, CHIP), CHIP)
            copies.append(pltpu.make_async_copy(parts[k], right.at[rows, :], sem.at[k]))
        for copy in copies:
            copy.start()
        for copy in copies:
            copy.wait()
        counts = jnp.dot(left_mask[...], right[:, SIDE * COLS :], preferred_element_type=F32)
        scale[...] = 1.0 / (counts + 0.001)

    value = left[...]
    for q in range(SIDE):
        part = jnp.dot(
            value, right[:, q * COLS : (q + 1) * COLS], preferred_element_type=F32
        ).astype(BF16)
        for i in range(block):
            at = i % beside * COLS
            outer[i // beside, q * SIDE : (q + 1) * SIDE, at : at + COLS] = part[
                i * SIDE : (i + 1) * SIDE
            ]
    first = pl.multiple_of(pl.program_id(0) * block, block)
    scales = scale[pl.ds(first, block), :]
    for i in range(0, block, beside):
        projected = jnp.dot(weight[...], outer[i // beside], preferred_element_type=F32)
        for k in range(beside):
            value = projected[:, k * COLS : (k + 1) * COLS] * scales[i + k : i + k + 1]
            out[i + k] = value.T.astype(BF16)


def pair(left, left_mask, weight, parts):
    block, beside = 8, 2
    whole = lambda a: pl.BlockSpec(a.shape, lambda i: (0,) * a.ndim)
    return pl.pallas_call(
        functools.partial(pair_kernel, block, beside),
        grid=(ROWS // block,),
        in_specs=[
            pl.BlockSpec((block * SIDE, TOTAL), lambda i: (i, 0)),
            whole(left_mask),
            whole(weight),
        ]
        + [pl.BlockSpec(memory_space=pl.ANY)] * len(parts),
        out_specs=pl.BlockSpec((block, COLS, PAIR), lambda i: (i, 0, 0)),
        out_shape=jax.ShapeDtypeStruct((ROWS, COLS, PAIR), BF16),
        scratch_shapes=[
            pltpu.VMEM((TOTAL, RIGHT), BF16),
            pltpu.VMEM((block // beside, SIDE * SIDE, beside * COLS), BF16),
            pltpu.VMEM((ROWS, COLS), F32),
            pltpu.SemaphoreType.DMA((RING,)),
        ],
        compiler_params=pltpu.CompilerParams(vmem_limit_bytes=40 * MEGA),
    )(left, left_mask, weight, *parts)


def local(
    homolog_embedding,
    sequence_row_mask,
    residue_chain_index,
    standardize_factor,
    standardize_shift,
    first_projector_matrix,
    second_projector_matrix,
    output_weight,
):
    own = project(
        homolog_embedding,
        sequence_row_mask,
        residue_chain_index,
        standardize_factor,
        standardize_shift,
        first_projector_matrix,
        second_projector_matrix,
    )
    along_y = [own[0]] + [res_shift(own[d], 0, d, 0) for d in range(1, RING)]
    far = res_shift(own[RING], 2, 0, 0)
    weight = arrange_weight(output_weight)
    along_y[2], weight = lax.optimization_barrier((along_y[2], weight))
    right, left, far_chip = stack(along_y + [core_swap(part) for part in along_y], far, core_swap(far))
    near = both_ways(right, 1, 0)
    left_parts = [to_row_owner(left, k) for k in range(2)]
    far_parts = [both_ways(far_chip, 0, 1), res_shift(far, 0, 2, 0)]
    left_parts, far_parts, near = lax.optimization_barrier((left_parts, far_parts, near))
    sides = arrange_left(left_parts + [core_swap(part) for part in left_parts])
    sides, far_chip = lax.optimization_barrier((sides, far_chip))
    far_right = stack_far(
        far_chip, far_parts[0], core_swap(far_parts[0]), far_parts[1], core_swap(far_parts[1])
    )
    return pair(*sides, weight, [right, near, core_swap(near), far_right])


def solution(mesh):
    in_specs = (P("res", "col", None), P("res", None), P("col"), P(), P(), P(), P(), P())
    out_specs = P("res", "col", None)
    return jax.shard_map(local, mesh=mesh, in_specs=in_specs, out_specs=out_specs, check_vma=False)
```

```python
import functools

import jax
import jax.numpy as jnp
from jax import lax
from jax.experimental import pallas as pl
from jax.experimental.pallas import tpu as pltpu
from jax.sharding import PartitionSpec as P

RING = 4
CORES = 2
SEQS = 4
EMBED = 256
SIDE = 32
PAIR = 128
COLS = 384
ROWS = 48
PLANE = ROWS * CORES
GROUP = SEQS * RING
CHIP = GROUP * CORES
TOTAL = CHIP * RING
LANES = 128
RIGHT = (SIDE + 1) * COLS
MAJOR, MINOR = 64, 32
LEFT = SIDE * PLANE + LANES
MEGA = 2**20
F32 = jnp.float32
BF16 = jnp.bfloat16


def position():
    res = lax.axis_index("res")
    return res // (RING * CORES), (res // CORES) % RING, res % CORES, lax.axis_index("col")


def res_shift(value, dz, dy, dc):
    pairs = []
    for r in range(RING * RING * CORES):
        z, y, c = r // (RING * CORES), (r // CORES) % RING, r % CORES
        to = (((z + dz) % RING) * RING + (y + dy) % RING) * CORES + (c + dc) % CORES
        pairs.append((r, to))
    return lax.ppermute(value, "res", pairs)


def core_swap(value):
    return res_shift(value, 0, 0, 1)


def both_ways(value, dz, dy):
    pairs = []
    for r in range(RING * RING * CORES):
        z, y, c = r // (RING * CORES), (r // CORES) % RING, r % CORES
        way = -1 if c else 1
        z, y = (z + way * dz) % RING, (y + way * dy) % RING
        pairs.append((r, (z * RING + y) * CORES + c))
    return lax.ppermute(value, "res", pairs)


def to_row_owner(value, k):
    pairs = []
    for z in range(RING):
        for y in range(RING):
            for c in range(CORES):
                for x in range(RING):
                    source = ((z * RING + y) * CORES + c) * RING + x
                    target = ((x * RING + y) * CORES + c) * RING + (z + k + 2 * c) % RING
                    pairs.append((source, target))
    return lax.ppermute(value, ("res", "col"), pairs)


def contract_last(a, b):
    return lax.dot_general(a, b, (((1,), (1,)), ((), ())), preferred_element_type=F32)


def side_by_side(value, count, start, width):
    rows = value.shape[0] // count
    lane = lax.broadcasted_iota(jnp.int32, (rows, LANES), 1)
    total = None
    for at in range(count):
        part = value[at * rows : (at + 1) * rows]
        move = (at * width - start) % LANES
        part = pltpu.roll(part, move, 1) if move else part
        total = part if total is None else jnp.where(lane >= at * width, part, total)
    return total


def project_kernel(*refs):
    arguments, outs = refs[:7], refs[7 : 8 + RING]
    emb, weights, chain, gain, shift, first, second = arguments
    both, right, left = refs[8 + RING :]
    _, y, _, _ = position()
    chains = weights.shape[1]
    ids = lax.broadcasted_iota(jnp.int32, (chains, COLS), 0)
    row = jnp.broadcast_to(chain[...].reshape(1, COLS), (chains, COLS))
    onehot = (row == ids).astype(F32).astype(BF16)
    mask = jnp.dot(weights[...], onehot, preferred_element_type=F32)
    both[0:SIDE] = first[...]
    both[SIDE:] = second[...]
    turn = lax.rem(RING - y, RING) * PLANE
    for s in range(SEQS):
        wide = emb[s].astype(F32)
        shifted = wide - jnp.mean(wide, axis=-1, keepdims=True)
        variance = jnp.mean(shifted * shifted, axis=-1, keepdims=True)
        value = shifted * lax.rsqrt(variance + 1e-05) * gain[...].reshape(1, EMBED)
        value = (value + shift[...].reshape(1, EMBED)).astype(BF16)
        sides = contract_last(both[...], value) * mask[s : s + 1]
        right[s] = sides[SIDE:]
        turned = pltpu.roll(sides[:SIDE], turn, 1)
        row = pltpu.roll(jnp.broadcast_to(mask[s : s + 1], (8, COLS)), turn, 1)
        fill = jnp.zeros((SIDE, LANES - PLANE), F32)
        for d in range(RING):
            part = jnp.concatenate([turned[:, d * PLANE : (d + 1) * PLANE], fill], 1)
            left[s, d, 0 : SIDE // 2] = side_by_side(part, 2, 0, MAJOR)
            left[s, d, SIDE // 2 : 3 * SIDE // 4] = side_by_side(part, 4, MAJOR, MINOR)
            part = jnp.concatenate([row[:, d * PLANE : (d + 1) * PLANE], fill[:8]], 1)
            left[s, d, 3 * SIDE // 4 :] = part
    for q in range(SIDE):
        part = right[:, q, :].astype(BF16)
        for out in outs:
            out[:, q * COLS : (q + 1) * COLS] = part
    for out in outs:
        out[:, SIDE * COLS : RIGHT] = mask.astype(BF16)
    for d, out in enumerate(outs[:RING]):
        for at in range(LEFT // LANES):
            to = RIGHT + at * LANES
            out[:, to : to + LANES] = left[:, d, at, :].astype(BF16)


def project(emb, weights, chain, gain, shift, first, second):
    arguments = (emb, weights, chain, gain, shift, first.T, second.T)
    return pl.pallas_call(
        project_kernel,
        in_specs=[pl.BlockSpec(memory_space=pltpu.VMEM)] * len(arguments),
        out_specs=[pl.BlockSpec(memory_space=pltpu.VMEM)] * (RING + 1),
        out_shape=[pltpu.VMEM((SEQS, RIGHT + LEFT), BF16)] * RING
        + [pltpu.VMEM((SEQS, RIGHT), BF16)],
        scratch_shapes=[
            pltpu.VMEM((2 * SIDE, EMBED), BF16),
            pltpu.VMEM((SEQS, SIDE, COLS), F32),
            pltpu.VMEM((SEQS, RING, LEFT // LANES + 7, LANES), F32),
        ],
        compiler_params=pltpu.CompilerParams(vmem_limit_bytes=60 * MEGA),
    )(*arguments)


def weight_kernel(weight_hbm, out, weight, wide, sem):
    copy = pltpu.make_async_copy(weight_hbm, weight, sem)
    copy.start()
    copy.wait()
    wide[...] = weight[...].astype(F32)
    for q in range(0, SIDE, 4):
        rows = [wide[pl.ds(q + at, SIDE, stride=SIDE), :] for at in range(4)]
        out[:, q * SIDE : (q + 4) * SIDE] = jnp.concatenate(rows, 0).T.astype(BF16)


def arrange_weight(weight):
    return pl.pallas_call(
        weight_kernel,
        in_specs=[pl.BlockSpec(memory_space=pl.ANY)],
        out_specs=pl.BlockSpec(memory_space=pltpu.VMEM),
        out_shape=jax.ShapeDtypeStruct((PAIR, SIDE * SIDE), BF16),
        scratch_shapes=[
            pltpu.VMEM((SIDE * SIDE, PAIR), BF16),
            pltpu.VMEM((SIDE * SIDE, PAIR), F32),
            pltpu.SemaphoreType.DMA,
        ],
        compiler_params=pltpu.CompilerParams(vmem_limit_bytes=16 * MEGA),
    )(weight)


def chunks(width):
    return [(at, min(2 * COLS, width - at)) for at in range(0, width, 2 * COLS)]


def by_core(core, own, other):
    return jnp.where(core == 0, own, other), jnp.where(core == 0, other, own)


def stack_kernel(*refs):
    parts, (right, left, wide) = refs[: RING * CORES], refs[RING * CORES :]
    _, _, core, _ = position()
    for out, base in ((left, RIGHT), (right, 0)):
        for at, width in chunks(out.shape[1]):
            lanes = slice(base + at, base + at + width)
            for c in range(CORES):
                start = pl.multiple_of(lax.rem(core + c, CORES) * GROUP, GROUP)
                half = wide.at[pl.ds(start, GROUP)]
                for d in range(RING):
                    half[d * SEQS : (d + 1) * SEQS, :width] = parts[c * RING + d][:, lanes].astype(F32)
            out[:, at : at + width] = wide[:, :width].astype(BF16)


def stack(parts):
    return pl.pallas_call(
        stack_kernel,
        out_shape=[
            jax.ShapeDtypeStruct((CHIP, RIGHT), BF16),
            jax.ShapeDtypeStruct((CHIP, LEFT), BF16),
        ],
        scratch_shapes=[pltpu.VMEM((CHIP, 2 * COLS), F32)],
        compiler_params=pltpu.CompilerParams(vmem_limit_bytes=16 * MEGA),
    )(*parts)


def chip_kernel(far, far_other, after, out, wide):
    _, _, core, _ = position()
    for at, width in chunks(RIGHT):
        lanes = slice(at, at + width)
        values = by_core(core, far[:, lanes].astype(F32), far_other[:, lanes].astype(F32))
        for c in range(CORES):
            wide[c * SEQS : (c + 1) * SEQS, :width] = values[c]
        out[:, lanes] = wide[:, :width].astype(BF16)


def stack_chip(far, far_other, after):
    vmem = pl.BlockSpec(memory_space=pltpu.VMEM)
    return pl.pallas_call(
        chip_kernel,
        in_specs=[vmem, vmem, pl.BlockSpec(memory_space=pl.ANY)],
        out_specs=vmem,
        out_shape=jax.ShapeDtypeStruct((CORES * SEQS, RIGHT), BF16),
        scratch_shapes=[pltpu.VMEM((CORES * SEQS, 2 * COLS), F32)],
        compiler_params=pltpu.CompilerParams(vmem_limit_bytes=16 * MEGA),
    )(far, far_other, after)


def far_kernel(own, near, near_other, far, far_other, right_part, _, right, wide, sem):
    _, _, core, _ = position()
    copy = pltpu.make_async_copy(right_part, right.at[rows_of(3 - 2 * core), :], sem)
    copy.start()
    for at, width in chunks(RIGHT):
        lanes = slice(at, at + width)
        below, above = by_core(core, near[:, lanes].astype(F32), near_other[:, lanes].astype(F32))
        opposite = by_core(core, far[:, lanes].astype(F32), far_other[:, lanes].astype(F32))
        here = own[:, lanes].astype(F32)
        for c in range(CORES):
            rows = slice(c * SEQS, (c + 1) * SEQS)
            for d, value in enumerate((here[rows], below[rows], opposite[c], above[rows])):
                start = c * GROUP + d * SEQS
                wide[start : start + SEQS, :width] = value
        right[2 * CHIP : 3 * CHIP, lanes] = wide[:, :width].astype(BF16)
    copy.wait()


def finish_right(parts, right_part, right):
    vmem, anywhere = (pl.BlockSpec(memory_space=m) for m in (pltpu.VMEM, pl.ANY))
    return pl.pallas_call(
        far_kernel,
        in_specs=[vmem] * len(parts) + [anywhere, vmem],
        out_specs=vmem,
        out_shape=pltpu.VMEM((TOTAL, RIGHT), BF16),
        input_output_aliases={len(parts) + 1: 0},
        scratch_shapes=[pltpu.VMEM((CHIP, 2 * COLS), F32), pltpu.SemaphoreType.DMA],
        compiler_params=pltpu.CompilerParams(vmem_limit_bytes=16 * MEGA),
    )(*parts, right_part, right)


def rows_of(slot):
    return pl.ds(pl.multiple_of(slot * CHIP, CHIP), CHIP)


def left_kernel(*refs):
    parts, (own, near, out, out_mask, right, stacked, turned, sem) = refs[:RING], refs[RING:]
    z, _, core, x = position()
    copies = [
        pltpu.make_async_copy(part, right.at[rows_of(slot), :], sem.at[k])
        for k, (part, slot) in enumerate(((own, 0), (near, 1 + 2 * core)))
    ]
    for copy in copies:
        copy.start()
    for at, part in enumerate(parts):
        group = lax.rem(z - x + at + 2 * core + RING, RING)
        stacked[pl.ds(pl.multiple_of(group * CHIP, CHIP), CHIP), :] = part[...]

    def block_at(at):
        return stacked[:, at * LANES : (at + 1) * LANES].astype(F32).T

    for p in range(SIDE // 2):
        block = block_at(p)
        for k in range(2):
            row = (p + k * SIDE // 2) * PLANE
            turned[row : row + MAJOR, :] = block[k * MAJOR : (k + 1) * MAJOR]
    for p in range(SIDE // 4):
        block = block_at(SIDE // 2 + p)
        for k in range(4):
            row = (p + k * SIDE // 4) * PLANE + MAJOR
            turned[row : row + MINOR, :] = block[k * MINOR : (k + 1) * MINOR]
    turned[SIDE * PLANE :, :] = block_at(3 * SIDE // 4)[:PLANE]
    base = core * ROWS
    for i in range(ROWS):
        rows = turned[pl.ds(base + i, SIDE, stride=PLANE), :]
        out[i * SIDE : (i + 1) * SIDE, :] = rows.astype(BF16)
    start = pl.multiple_of(SIDE * PLANE + base, 8)
    out_mask[...] = turned[pl.ds(start, ROWS), :].astype(BF16)
    for copy in copies:
        copy.wait()


def arrange_left(parts, own, near):
    vmem, anywhere = (pl.BlockSpec(memory_space=m) for m in (pltpu.VMEM, pl.ANY))
    return pl.pallas_call(
        left_kernel,
        in_specs=[vmem] * len(parts) + [anywhere] * 2,
        out_specs=[vmem] * 3,
        out_shape=[
            jax.ShapeDtypeStruct((ROWS * SIDE, TOTAL), BF16),
            jax.ShapeDtypeStruct((ROWS, TOTAL), BF16),
            pltpu.VMEM((TOTAL, RIGHT), BF16),
        ],
        scratch_shapes=[
            pltpu.VMEM((TOTAL, LEFT), BF16),
            pltpu.VMEM(((SIDE + 1) * PLANE, TOTAL), F32),
            pltpu.SemaphoreType.DMA((2,)),
        ],
        compiler_params=pltpu.CompilerParams(vmem_limit_bytes=16 * MEGA),
    )(*parts, own, near)


def pair_kernel(block, beside, left, left_mask, weight, right, out, outer, scale):
    @pl.when(pl.program_id(0) == 0)
    def _():
        counts = jnp.dot(left_mask[...], right[:, SIDE * COLS :], preferred_element_type=F32)
        scale[...] = 1.0 / (counts + 0.001)

    value = left[...]
    for q in range(SIDE):
        part = jnp.dot(
            value, right[:, q * COLS : (q + 1) * COLS], preferred_element_type=F32
        ).astype(BF16)
        for i in range(block):
            at = i % beside * COLS
            outer[i // beside, q * SIDE : (q + 1) * SIDE, at : at + COLS] = part[
                i * SIDE : (i + 1) * SIDE
            ]
    first = pl.multiple_of(pl.program_id(0) * block, block)
    scales = scale[pl.ds(first, block), :]
    for i in range(0, block, beside):
        projected = jnp.dot(weight[...], outer[i // beside], preferred_element_type=F32)
        for k in range(beside):
            value = projected[:, k * COLS : (k + 1) * COLS] * scales[i + k : i + k + 1]
            out[i + k] = value.T.astype(BF16)


def pair(left, left_mask, weight, right):
    block, beside = 16, 2
    whole = lambda a: pl.BlockSpec(a.shape, lambda i: (0,) * a.ndim)
    return pl.pallas_call(
        functools.partial(pair_kernel, block, beside),
        grid=(ROWS // block,),
        in_specs=[
            pl.BlockSpec((block * SIDE, TOTAL), lambda i: (i, 0)),
            whole(left_mask),
            whole(weight),
            pl.BlockSpec(memory_space=pltpu.VMEM),
        ],
        out_specs=pl.BlockSpec((block, COLS, PAIR), lambda i: (i, 0, 0)),
        out_shape=jax.ShapeDtypeStruct((ROWS, COLS, PAIR), BF16),
        scratch_shapes=[
            pltpu.VMEM((block // beside, SIDE * SIDE, beside * COLS), BF16),
            pltpu.VMEM((ROWS, COLS), F32),
        ],
        compiler_params=pltpu.CompilerParams(vmem_limit_bytes=40 * MEGA),
    )(left, left_mask, weight, right)


def local(
    homolog_embedding,
    sequence_row_mask,
    residue_chain_index,
    standardize_factor,
    standardize_shift,
    first_projector_matrix,
    second_projector_matrix,
    output_weight,
):
    own = project(
        homolog_embedding,
        sequence_row_mask,
        residue_chain_index,
        standardize_factor,
        standardize_shift,
        first_projector_matrix,
        second_projector_matrix,
    )
    along_y = [own[0]] + [res_shift(own[d], 0, d, 0) for d in range(1, RING)]
    far = res_shift(own[RING], 2, 0, 0)
    weight = arrange_weight(output_weight)
    along_y[2], weight = lax.optimization_barrier((along_y[2], weight))
    along_y[3], far = lax.optimization_barrier((along_y[3], far))
    swapped = [core_swap(part) for part in along_y]
    right, left = stack(along_y + swapped)
    left_parts = [to_row_owner(left, k) for k in range(2)]
    near = both_ways(right, 1, 0)
    far_chip = stack_chip(far, core_swap(far), left)
    far_parts = [both_ways(far_chip, 0, 1), res_shift(far, 0, 2, 0)]
    left_parts, far_parts, near = lax.optimization_barrier((left_parts, far_parts, near))
    left_others = [core_swap(part) for part in left_parts]
    far_others = [core_swap(part) for part in far_parts]
    left_others, far_others, near = lax.optimization_barrier((left_others, far_others, near))
    left_all, left_mask, right_all = arrange_left(left_parts + left_others, right, near)
    far_parts = [far_chip, far_parts[0], far_others[0], far_parts[1], far_others[1]]
    right_all = finish_right(far_parts, core_swap(near), right_all)
    return pair(left_all, left_mask, weight, right_all)


def solution(mesh):
    in_specs = (P("res", "col", None), P("res", None), P("col"), P(), P(), P(), P(), P())
    out_specs = P("res", "col", None)
    return jax.shard_map(local, mesh=mesh, in_specs=in_specs, out_specs=out_specs, check_vma=False)
```

```python
import functools

import jax
import jax.numpy as jnp
from jax import lax
from jax.experimental import pallas as pl
from jax.experimental.pallas import tpu as pltpu
from jax.sharding import PartitionSpec as P

RING = 4
CORES = 2
SEQS = 4
EMBED = 256
SIDE = 32
PAIR = 128
COLS = 384
ROWS = 48
PLANE = ROWS * CORES
GROUP = SEQS * RING
CHIP = GROUP * CORES
TOTAL = CHIP * RING
LANES = 128
RIGHT = (SIDE + 1) * COLS
MAJOR, MINOR = 64, 32
LEFT = SIDE * PLANE + LANES
MEGA = 2**20
F32 = jnp.float32
BF16 = jnp.bfloat16


def position():
    res = lax.axis_index("res")
    return res // (RING * CORES), (res // CORES) % RING, res % CORES, lax.axis_index("col")


def res_shift(value, dz, dy, dc):
    pairs = []
    for r in range(RING * RING * CORES):
        z, y, c = r // (RING * CORES), (r // CORES) % RING, r % CORES
        to = (((z + dz) % RING) * RING + (y + dy) % RING) * CORES + (c + dc) % CORES
        pairs.append((r, to))
    return lax.ppermute(value, "res", pairs)


def core_swap(value):
    return res_shift(value, 0, 0, 1)


def both_ways(value, dz, dy):
    pairs = []
    for r in range(RING * RING * CORES):
        z, y, c = r // (RING * CORES), (r // CORES) % RING, r % CORES
        way = -1 if c else 1
        z, y = (z + way * dz) % RING, (y + way * dy) % RING
        pairs.append((r, (z * RING + y) * CORES + c))
    return lax.ppermute(value, "res", pairs)


def to_row_owner(value, k):
    pairs = []
    for z in range(RING):
        for y in range(RING):
            for c in range(CORES):
                for x in range(RING):
                    source = ((z * RING + y) * CORES + c) * RING + x
                    target = ((x * RING + y) * CORES + c) * RING + (z + k + 2 * c) % RING
                    pairs.append((source, target))
    return lax.ppermute(value, ("res", "col"), pairs)


def contract_last(a, b):
    return lax.dot_general(a, b, (((1,), (1,)), ((), ())), preferred_element_type=F32)


def side_by_side(value, count, start, width):
    rows = value.shape[0] // count
    lane = lax.broadcasted_iota(jnp.int32, (rows, LANES), 1)
    total = None
    for at in range(count):
        part = value[at * rows : (at + 1) * rows]
        move = (at * width - start) % LANES
        part = pltpu.roll(part, move, 1) if move else part
        total = part if total is None else jnp.where(lane >= at * width, part, total)
    return total


def project_kernel(*refs):
    arguments, outs = refs[:7], refs[7 : 8 + RING]
    emb, weights, chain, gain, shift, first, second = arguments
    both, right, left = refs[8 + RING :]
    _, y, _, _ = position()
    chains = weights.shape[1]
    ids = lax.broadcasted_iota(jnp.int32, (chains, COLS), 0)
    row = jnp.broadcast_to(chain[...].reshape(1, COLS), (chains, COLS))
    onehot = (row == ids).astype(F32).astype(BF16)
    mask = jnp.dot(weights[...], onehot, preferred_element_type=F32)
    both[0:SIDE] = first[...]
    both[SIDE:] = second[...]
    turn = lax.rem(RING - y, RING) * PLANE
    for s in range(SEQS):
        wide = emb[s].astype(F32)
        shifted = wide - jnp.mean(wide, axis=-1, keepdims=True)
        variance = jnp.mean(shifted * shifted, axis=-1, keepdims=True)
        value = shifted * lax.rsqrt(variance + 1e-05) * gain[...].reshape(1, EMBED)
        value = (value + shift[...].reshape(1, EMBED)).astype(BF16)
        sides = contract_last(both[...], value) * mask[s : s + 1]
        right[s] = sides[SIDE:]
        turned = pltpu.roll(sides[:SIDE], turn, 1)
        row = pltpu.roll(jnp.broadcast_to(mask[s : s + 1], (8, COLS)), turn, 1)
        fill = jnp.zeros((SIDE, LANES - PLANE), F32)
        for d in range(RING):
            part = jnp.concatenate([turned[:, d * PLANE : (d + 1) * PLANE], fill], 1)
            left[s, d, 0 : SIDE // 2] = side_by_side(part, 2, 0, MAJOR)
            left[s, d, SIDE // 2 : 3 * SIDE // 4] = side_by_side(part, 4, MAJOR, MINOR)
            part = jnp.concatenate([row[:, d * PLANE : (d + 1) * PLANE], fill[:8]], 1)
            left[s, d, 3 * SIDE // 4 :] = part
    for q in range(SIDE):
        part = right[:, q, :].astype(BF16)
        for out in outs:
            out[:, q * COLS : (q + 1) * COLS] = part
    for out in outs:
        out[:, SIDE * COLS : RIGHT] = mask.astype(BF16)
    for d, out in enumerate(outs[:RING]):
        for at in range(LEFT // LANES):
            to = RIGHT + at * LANES
            out[:, to : to + LANES] = left[:, d, at, :].astype(BF16)


def project(emb, weights, chain, gain, shift, first, second):
    arguments = (emb, weights, chain, gain, shift, first.T, second.T)
    return pl.pallas_call(
        project_kernel,
        in_specs=[pl.BlockSpec(memory_space=pltpu.VMEM)] * len(arguments),
        out_specs=[pl.BlockSpec(memory_space=pltpu.VMEM)] * (RING + 1),
        out_shape=[pltpu.VMEM((SEQS, RIGHT + LEFT), BF16)] * RING
        + [pltpu.VMEM((SEQS, RIGHT), BF16)],
        scratch_shapes=[
            pltpu.VMEM((2 * SIDE, EMBED), BF16),
            pltpu.VMEM((SEQS, SIDE, COLS), F32),
            pltpu.VMEM((SEQS, RING, LEFT // LANES + 7, LANES), F32),
        ],
        compiler_params=pltpu.CompilerParams(vmem_limit_bytes=60 * MEGA),
    )(*arguments)


def weight_kernel(weight_hbm, out, weight, wide, sem):
    copy = pltpu.make_async_copy(weight_hbm, weight, sem)
    copy.start()
    copy.wait()
    wide[...] = weight[...].astype(F32)
    for q in range(0, SIDE, 4):
        rows = [wide[pl.ds(q + at, SIDE, stride=SIDE), :] for at in range(4)]
        out[:, q * SIDE : (q + 4) * SIDE] = jnp.concatenate(rows, 0).T.astype(BF16)


def arrange_weight(weight):
    return pl.pallas_call(
        weight_kernel,
        in_specs=[pl.BlockSpec(memory_space=pl.ANY)],
        out_specs=pl.BlockSpec(memory_space=pltpu.VMEM),
        out_shape=jax.ShapeDtypeStruct((PAIR, SIDE * SIDE), BF16),
        scratch_shapes=[
            pltpu.VMEM((SIDE * SIDE, PAIR), BF16),
            pltpu.VMEM((SIDE * SIDE, PAIR), F32),
            pltpu.SemaphoreType.DMA,
        ],
        compiler_params=pltpu.CompilerParams(vmem_limit_bytes=16 * MEGA),
    )(weight)


def chunks(width):
    return [(at, min(2 * COLS, width - at)) for at in range(0, width, 2 * COLS)]


def by_core(core, own, other):
    return jnp.where(core == 0, own, other), jnp.where(core == 0, other, own)


def stack_kernel(*refs):
    parts, (right, left, wide) = refs[: RING * CORES], refs[RING * CORES :]
    _, _, core, _ = position()
    for out, base in ((left, RIGHT), (right, 0)):
        for at, width in chunks(out.shape[1]):
            lanes = slice(base + at, base + at + width)
            for c in range(CORES):
                start = pl.multiple_of(lax.rem(core + c, CORES) * GROUP, GROUP)
                half = wide.at[pl.ds(start, GROUP)]
                for d in range(RING):
                    half[d * SEQS : (d + 1) * SEQS, :width] = parts[c * RING + d][:, lanes].astype(F32)
            out[:, at : at + width] = wide[:, :width].astype(BF16)


def stack(parts):
    return pl.pallas_call(
        stack_kernel,
        out_shape=[
            jax.ShapeDtypeStruct((CHIP, RIGHT), BF16),
            jax.ShapeDtypeStruct((CHIP, LEFT), BF16),
        ],
        scratch_shapes=[pltpu.VMEM((CHIP, 2 * COLS), F32)],
        compiler_params=pltpu.CompilerParams(vmem_limit_bytes=16 * MEGA),
    )(*parts)


def chip_kernel(far, far_other, after, out, wide):
    _, _, core, _ = position()
    for at, width in chunks(RIGHT):
        lanes = slice(at, at + width)
        values = by_core(core, far[:, lanes].astype(F32), far_other[:, lanes].astype(F32))
        for c in range(CORES):
            wide[c * SEQS : (c + 1) * SEQS, :width] = values[c]
        out[:, lanes] = wide[:, :width].astype(BF16)


def stack_chip(far, far_other, after):
    vmem = pl.BlockSpec(memory_space=pltpu.VMEM)
    return pl.pallas_call(
        chip_kernel,
        in_specs=[vmem, vmem, pl.BlockSpec(memory_space=pl.ANY)],
        out_specs=vmem,
        out_shape=jax.ShapeDtypeStruct((CORES * SEQS, RIGHT), BF16),
        scratch_shapes=[pltpu.VMEM((CORES * SEQS, 2 * COLS), F32)],
        compiler_params=pltpu.CompilerParams(vmem_limit_bytes=16 * MEGA),
    )(far, far_other, after)


def stack_far(own, near, near_other, far, far_other, out, wide):
    core = position()[2]
    for at, width in chunks(RIGHT):
        lanes = slice(at, at + width)
        below, above = by_core(core, near[:, lanes].astype(F32), near_other[:, lanes].astype(F32))
        opposite = by_core(core, far[:, lanes].astype(F32), far_other[:, lanes].astype(F32))
        here = own[:, lanes].astype(F32)
        for c in range(CORES):
            rows = slice(c * SEQS, (c + 1) * SEQS)
            for d, value in enumerate((here[rows], below[rows], opposite[c], above[rows])):
                start = c * GROUP + d * SEQS
                wide[start : start + SEQS, :width] = value
        out[2 * CHIP : 3 * CHIP, lanes] = wide[:, :width].astype(BF16)


def finish_kernel(right_part, _, right, sem):
    core = position()[2]
    copy = pltpu.make_async_copy(right_part, right.at[rows_of(3 - 2 * core), :], sem)
    copy.start()
    copy.wait()


def finish_right(right_part, right):
    vmem, anywhere = (pl.BlockSpec(memory_space=m) for m in (pltpu.VMEM, pl.ANY))
    return pl.pallas_call(
        finish_kernel,
        in_specs=[anywhere, vmem],
        out_specs=vmem,
        out_shape=pltpu.VMEM((TOTAL, RIGHT), BF16),
        input_output_aliases={1: 0},
        scratch_shapes=[pltpu.SemaphoreType.DMA],
        compiler_params=pltpu.CompilerParams(vmem_limit_bytes=16 * MEGA),
    )(right_part, right)


def rows_of(slot):
    return pl.ds(pl.multiple_of(slot * CHIP, CHIP), CHIP)


def left_kernel(*refs):
    parts, fars, refs = refs[:RING], refs[RING : RING + 5], refs[RING + 5 :]
    own, near, out, out_mask, right, stacked, turned, wide, sem = refs
    z, _, core, x = position()
    copies = [
        pltpu.make_async_copy(part, right.at[rows_of(slot), :], sem.at[k])
        for k, (part, slot) in enumerate(((own, 0), (near, 1 + 2 * core)))
    ]
    for copy in copies:
        copy.start()
    for at, part in enumerate(parts):
        group = lax.rem(z - x + at + 2 * core + RING, RING)
        stacked[pl.ds(pl.multiple_of(group * CHIP, CHIP), CHIP), :] = part[...]

    def block_at(at):
        return stacked[:, at * LANES : (at + 1) * LANES].astype(F32).T

    for p in range(SIDE // 2):
        block = block_at(p)
        for k in range(2):
            row = (p + k * SIDE // 2) * PLANE
            turned[row : row + MAJOR, :] = block[k * MAJOR : (k + 1) * MAJOR]
    for p in range(SIDE // 4):
        block = block_at(SIDE // 2 + p)
        for k in range(4):
            row = (p + k * SIDE // 4) * PLANE + MAJOR
            turned[row : row + MINOR, :] = block[k * MINOR : (k + 1) * MINOR]
    turned[SIDE * PLANE :, :] = block_at(3 * SIDE // 4)[:PLANE]
    base = core * ROWS
    for i in range(ROWS):
        rows = turned[pl.ds(base + i, SIDE, stride=PLANE), :]
        out[i * SIDE : (i + 1) * SIDE, :] = rows.astype(BF16)
    start = pl.multiple_of(SIDE * PLANE + base, 8)
    out_mask[...] = turned[pl.ds(start, ROWS), :].astype(BF16)
    stack_far(*fars, right, wide)
    for copy in copies:
        copy.wait()


def arrange_left(parts, fars, own, near):
    vmem, anywhere = (pl.BlockSpec(memory_space=m) for m in (pltpu.VMEM, pl.ANY))
    return pl.pallas_call(
        left_kernel,
        in_specs=[vmem] * (len(parts) + len(fars)) + [anywhere] * 2,
        out_specs=[vmem] * 3,
        out_shape=[
            jax.ShapeDtypeStruct((ROWS * SIDE, TOTAL), BF16),
            jax.ShapeDtypeStruct((ROWS, TOTAL), BF16),
            pltpu.VMEM((TOTAL, RIGHT), BF16),
        ],
        scratch_shapes=[
            pltpu.VMEM((TOTAL, LEFT), BF16),
            pltpu.VMEM(((SIDE + 1) * PLANE, TOTAL), F32),
            pltpu.VMEM((CHIP, 2 * COLS), F32),
            pltpu.SemaphoreType.DMA((2,)),
        ],
        compiler_params=pltpu.CompilerParams(vmem_limit_bytes=16 * MEGA),
    )(*parts, *fars, own, near)


def pair_kernel(block, beside, left, left_mask, weight, right, out, outer, scale):
    @pl.when(pl.program_id(0) == 0)
    def _():
        counts = jnp.dot(left_mask[...], right[:, SIDE * COLS :], preferred_element_type=F32)
        scale[...] = 1.0 / (counts + 0.001)

    value = left[...]
    for q in range(SIDE):
        part = jnp.dot(
            value, right[:, q * COLS : (q + 1) * COLS], preferred_element_type=F32
        ).astype(BF16)
        for i in range(block):
            at = i % beside * COLS
            outer[i // beside, q * SIDE : (q + 1) * SIDE, at : at + COLS] = part[
                i * SIDE : (i + 1) * SIDE
            ]
    first = pl.multiple_of(pl.program_id(0) * block, block)
    scales = scale[pl.ds(first, block), :]
    for i in range(0, block, beside):
        projected = jnp.dot(weight[...], outer[i // beside], preferred_element_type=F32)
        for k in range(beside):
            value = projected[:, k * COLS : (k + 1) * COLS] * scales[i + k : i + k + 1]
            out[i + k] = value.T.astype(BF16)


def pair(left, left_mask, weight, right):
    block, beside = 16, 2
    whole = lambda a: pl.BlockSpec(a.shape, lambda i: (0,) * a.ndim)
    return pl.pallas_call(
        functools.partial(pair_kernel, block, beside),
        grid=(ROWS // block,),
        in_specs=[
            pl.BlockSpec((block * SIDE, TOTAL), lambda i: (i, 0)),
            whole(left_mask),
            whole(weight),
            pl.BlockSpec(memory_space=pltpu.VMEM),
        ],
        out_specs=pl.BlockSpec((block, COLS, PAIR), lambda i: (i, 0, 0)),
        out_shape=jax.ShapeDtypeStruct((ROWS, COLS, PAIR), BF16),
        scratch_shapes=[
            pltpu.VMEM((block // beside, SIDE * SIDE, beside * COLS), BF16),
            pltpu.VMEM((ROWS, COLS), F32),
        ],
        compiler_params=pltpu.CompilerParams(vmem_limit_bytes=40 * MEGA),
    )(left, left_mask, weight, right)


def local(
    homolog_embedding,
    sequence_row_mask,
    residue_chain_index,
    standardize_factor,
    standardize_shift,
    first_projector_matrix,
    second_projector_matrix,
    output_weight,
):
    own = project(
        homolog_embedding,
        sequence_row_mask,
        residue_chain_index,
        standardize_factor,
        standardize_shift,
        first_projector_matrix,
        second_projector_matrix,
    )
    along_y = [own[0]] + [res_shift(own[d], 0, d, 0) for d in range(1, RING)]
    far = res_shift(own[RING], 2, 0, 0)
    weight = arrange_weight(output_weight)
    along_y[2], weight = lax.optimization_barrier((along_y[2], weight))
    along_y[3], far = lax.optimization_barrier((along_y[3], far))
    swapped = [core_swap(part) for part in along_y]
    right, left = stack(along_y + swapped)
    left_parts = [to_row_owner(left, k) for k in range(2)]
    near = both_ways(right, 1, 0)
    far_chip = stack_chip(far, core_swap(far), left)
    far_parts = [both_ways(far_chip, 0, 1), res_shift(far, 0, 2, 0)]
    left_parts, far_parts, near = lax.optimization_barrier((left_parts, far_parts, near))
    left_others = [core_swap(part) for part in left_parts]
    far_others = [core_swap(part) for part in far_parts]
    left_others, far_others, near = lax.optimization_barrier((left_others, far_others, near))
    far_parts = [far_chip, far_parts[0], far_others[0], far_parts[1], far_others[1]]
    left_parts = left_parts + left_others
    left_all, left_mask, right_all = arrange_left(left_parts, far_parts, right, near)
    right_all = finish_right(core_swap(near), right_all)
    return pair(left_all, left_mask, weight, right_all)


def solution(mesh):
    in_specs = (P("res", "col", None), P("res", None), P("col"), P(), P(), P(), P(), P())
    out_specs = P("res", "col", None)
    return jax.shard_map(local, mesh=mesh, in_specs=in_specs, out_specs=out_specs, check_vma=False)
```

```python
import functools

import jax
import jax.numpy as jnp
from jax import lax
from jax.experimental import pallas as pl
from jax.experimental.pallas import tpu as pltpu
from jax.sharding import PartitionSpec as P

RING = 4
CORES = 2
SEQS = 4
EMBED = 256
SIDE = 32
PAIR = 128
COLS = 384
ROWS = 48
PLANE = ROWS * CORES
GROUP = SEQS * RING
CHIP = GROUP * CORES
TOTAL = CHIP * RING
LANES = 128
RIGHT = (SIDE + 1) * COLS
MAJOR, MINOR = 64, 32
LEFT = SIDE * PLANE + LANES
MEGA = 2**20
F32 = jnp.float32
BF16 = jnp.bfloat16


def position():
    res = lax.axis_index("res")
    return res // (RING * CORES), (res // CORES) % RING, res % CORES, lax.axis_index("col")


def res_shift(value, dz, dy, dc):
    pairs = []
    for r in range(RING * RING * CORES):
        z, y, c = r // (RING * CORES), (r // CORES) % RING, r % CORES
        to = (((z + dz) % RING) * RING + (y + dy) % RING) * CORES + (c + dc) % CORES
        pairs.append((r, to))
    return lax.ppermute(value, "res", pairs)


def core_swap(value):
    return res_shift(value, 0, 0, 1)


def both_ways(value, dz, dy):
    pairs = []
    for r in range(RING * RING * CORES):
        z, y, c = r // (RING * CORES), (r // CORES) % RING, r % CORES
        way = -1 if c else 1
        z, y = (z + way * dz) % RING, (y + way * dy) % RING
        pairs.append((r, (z * RING + y) * CORES + c))
    return lax.ppermute(value, "res", pairs)


def to_row_owner(value, k):
    pairs = []
    for z in range(RING):
        for y in range(RING):
            for c in range(CORES):
                for x in range(RING):
                    source = ((z * RING + y) * CORES + c) * RING + x
                    target = ((x * RING + y) * CORES + c) * RING + (z ^ x ^ (k + 2 * c))
                    pairs.append((source, target))
    return lax.ppermute(value, ("res", "col"), pairs)


def contract_last(a, b):
    return lax.dot_general(a, b, (((1,), (1,)), ((), ())), preferred_element_type=F32)


def side_by_side(value, count, start, width):
    rows = value.shape[0] // count
    lane = lax.broadcasted_iota(jnp.int32, (rows, LANES), 1)
    total = None
    for at in range(count):
        part = value[at * rows : (at + 1) * rows]
        move = (at * width - start) % LANES
        part = pltpu.roll(part, move, 1) if move else part
        total = part if total is None else jnp.where(lane >= at * width, part, total)
    return total


def project_kernel(*refs):
    arguments, outs = refs[:7], refs[7 : 8 + RING]
    emb, weights, chain, gain, shift, first, second = arguments
    both, right, left = refs[8 + RING :]
    _, y, _, _ = position()
    chains = weights.shape[1]
    ids = lax.broadcasted_iota(jnp.int32, (chains, COLS), 0)
    row = jnp.broadcast_to(chain[...].reshape(1, COLS), (chains, COLS))
    onehot = (row == ids).astype(F32).astype(BF16)
    mask = jnp.dot(weights[...], onehot, preferred_element_type=F32)
    both[0:SIDE] = first[...]
    both[SIDE:] = second[...]
    turn = lax.rem(RING - y, RING) * PLANE
    for s in range(SEQS):
        wide = emb[s].astype(F32)
        shifted = wide - jnp.mean(wide, axis=-1, keepdims=True)
        variance = jnp.mean(shifted * shifted, axis=-1, keepdims=True)
        value = shifted * lax.rsqrt(variance + 1e-05) * gain[...].reshape(1, EMBED)
        value = (value + shift[...].reshape(1, EMBED)).astype(BF16)
        sides = contract_last(both[...], value) * mask[s : s + 1]
        right[s] = sides[SIDE:]
        turned = pltpu.roll(sides[:SIDE], turn, 1)
        row = pltpu.roll(jnp.broadcast_to(mask[s : s + 1], (8, COLS)), turn, 1)
        fill = jnp.zeros((SIDE, LANES - PLANE), F32)
        for d in range(RING):
            part = jnp.concatenate([turned[:, d * PLANE : (d + 1) * PLANE], fill], 1)
            left[s, d, 0 : SIDE // 2] = side_by_side(part, 2, 0, MAJOR)
            left[s, d, SIDE // 2 : 3 * SIDE // 4] = side_by_side(part, 4, MAJOR, MINOR)
            part = jnp.concatenate([row[:, d * PLANE : (d + 1) * PLANE], fill[:8]], 1)
            left[s, d, 3 * SIDE // 4 :] = part
    for q in range(SIDE):
        part = right[:, q, :].astype(BF16)
        for out in outs:
            out[:, q * COLS : (q + 1) * COLS] = part
    for out in outs:
        out[:, SIDE * COLS : RIGHT] = mask.astype(BF16)
    for d, out in enumerate(outs[:RING]):
        for at in range(LEFT // LANES):
            to = RIGHT + at * LANES
            out[:, to : to + LANES] = left[:, d, at, :].astype(BF16)


def project(emb, weights, chain, gain, shift, first, second):
    arguments = (emb, weights, chain, gain, shift, first.T, second.T)
    return pl.pallas_call(
        project_kernel,
        in_specs=[pl.BlockSpec(memory_space=pltpu.VMEM)] * len(arguments),
        out_specs=[pl.BlockSpec(memory_space=pltpu.VMEM)] * (RING + 1),
        out_shape=[pltpu.VMEM((SEQS, RIGHT + LEFT), BF16)] * RING
        + [pltpu.VMEM((SEQS, RIGHT), BF16)],
        scratch_shapes=[
            pltpu.VMEM((2 * SIDE, EMBED), BF16),
            pltpu.VMEM((SEQS, SIDE, COLS), F32),
            pltpu.VMEM((SEQS, RING, LEFT // LANES + 7, LANES), F32),
        ],
        compiler_params=pltpu.CompilerParams(vmem_limit_bytes=60 * MEGA),
    )(*arguments)


def weight_kernel(weight_hbm, out, weight, wide, sem):
    copy = pltpu.make_async_copy(weight_hbm, weight, sem)
    copy.start()
    copy.wait()
    wide[...] = weight[...].astype(F32)
    for q in range(0, SIDE, 4):
        rows = [wide[pl.ds(q + at, SIDE, stride=SIDE), :] for at in range(4)]
        out[:, q * SIDE : (q + 4) * SIDE] = jnp.concatenate(rows, 0).T.astype(BF16)


def arrange_weight(weight):
    return pl.pallas_call(
        weight_kernel,
        in_specs=[pl.BlockSpec(memory_space=pl.ANY)],
        out_specs=pl.BlockSpec(memory_space=pltpu.VMEM),
        out_shape=jax.ShapeDtypeStruct((PAIR, SIDE * SIDE), BF16),
        scratch_shapes=[
            pltpu.VMEM((SIDE * SIDE, PAIR), BF16),
            pltpu.VMEM((SIDE * SIDE, PAIR), F32),
            pltpu.SemaphoreType.DMA,
        ],
        compiler_params=pltpu.CompilerParams(vmem_limit_bytes=16 * MEGA),
    )(weight)


def chunks(width):
    return [(at, min(2 * COLS, width - at)) for at in range(0, width, 2 * COLS)]


def by_core(core, own, other):
    return jnp.where(core == 0, own, other), jnp.where(core == 0, other, own)


def stack_kernel(*refs):
    parts, (right, left, wide) = refs[: RING * CORES], refs[RING * CORES :]
    _, _, core, _ = position()
    for out, base in ((left, RIGHT), (right, 0)):
        for at, width in chunks(out.shape[1]):
            lanes = slice(base + at, base + at + width)
            for c in range(CORES):
                start = pl.multiple_of(lax.rem(core + c, CORES) * GROUP, GROUP)
                half = wide.at[pl.ds(start, GROUP)]
                for d in range(RING):
                    half[d * SEQS : (d + 1) * SEQS, :width] = parts[c * RING + d][:, lanes].astype(F32)
            out[:, at : at + width] = wide[:, :width].astype(BF16)


def stack(parts):
    return pl.pallas_call(
        stack_kernel,
        out_shape=[
            jax.ShapeDtypeStruct((CHIP, RIGHT), BF16),
            jax.ShapeDtypeStruct((CHIP, LEFT), BF16),
        ],
        scratch_shapes=[pltpu.VMEM((CHIP, 2 * COLS), F32)],
        compiler_params=pltpu.CompilerParams(vmem_limit_bytes=16 * MEGA),
    )(*parts)


def chip_kernel(far, far_other, after, out, wide):
    _, _, core, _ = position()
    for at, width in chunks(RIGHT):
        lanes = slice(at, at + width)
        values = by_core(core, far[:, lanes].astype(F32), far_other[:, lanes].astype(F32))
        for c in range(CORES):
            wide[c * SEQS : (c + 1) * SEQS, :width] = values[c]
        out[:, lanes] = wide[:, :width].astype(BF16)


def stack_chip(far, far_other, after):
    vmem = pl.BlockSpec(memory_space=pltpu.VMEM)
    return pl.pallas_call(
        chip_kernel,
        in_specs=[vmem, vmem, pl.BlockSpec(memory_space=pl.ANY)],
        out_specs=vmem,
        out_shape=jax.ShapeDtypeStruct((CORES * SEQS, RIGHT), BF16),
        scratch_shapes=[pltpu.VMEM((CORES * SEQS, 2 * COLS), F32)],
        compiler_params=pltpu.CompilerParams(vmem_limit_bytes=16 * MEGA),
    )(far, far_other, after)


def stack_far(own, near, near_other, far, far_other, out, wide):
    core = position()[2]
    for at, width in chunks(RIGHT):
        lanes = slice(at, at + width)
        below, above = by_core(core, near[:, lanes].astype(F32), near_other[:, lanes].astype(F32))
        opposite = by_core(core, far[:, lanes].astype(F32), far_other[:, lanes].astype(F32))
        here = own[:, lanes].astype(F32)
        for c in range(CORES):
            rows = slice(c * SEQS, (c + 1) * SEQS)
            for d, value in enumerate((here[rows], below[rows], opposite[c], above[rows])):
                start = c * GROUP + d * SEQS
                wide[start : start + SEQS, :width] = value
        out[2 * CHIP : 3 * CHIP, lanes] = wide[:, :width].astype(BF16)


def finish_kernel(right_part, _, right, sem):
    core = position()[2]
    copy = pltpu.make_async_copy(right_part, right.at[rows_of(3 - 2 * core), :], sem)
    copy.start()
    copy.wait()


def finish_right(right_part, right):
    vmem, anywhere = (pl.BlockSpec(memory_space=m) for m in (pltpu.VMEM, pl.ANY))
    return pl.pallas_call(
        finish_kernel,
        in_specs=[anywhere, vmem],
        out_specs=vmem,
        out_shape=pltpu.VMEM((TOTAL, RIGHT), BF16),
        input_output_aliases={1: 0},
        scratch_shapes=[pltpu.SemaphoreType.DMA],
        compiler_params=pltpu.CompilerParams(vmem_limit_bytes=16 * MEGA),
    )(right_part, right)


def rows_of(slot):
    return pl.ds(pl.multiple_of(slot * CHIP, CHIP), CHIP)


def left_kernel(*refs):
    parts, fars, refs = refs[:RING], refs[RING : RING + 5], refs[RING + 5 :]
    own, near, out, out_mask, right, stacked, turned, wide, sem = refs
    z, _, core, x = position()
    copies = [
        pltpu.make_async_copy(part, right.at[rows_of(slot), :], sem.at[k])
        for k, (part, slot) in enumerate(((own, 0), (near, 1 + 2 * core)))
    ]
    for copy in copies:
        copy.start()
    for at, part in enumerate(parts):
        source = z ^ x ^ lax.rem(at + 2 * core, RING)
        group = lax.rem(z - source + RING, RING)
        stacked[pl.ds(pl.multiple_of(group * CHIP, CHIP), CHIP), :] = part[...]

    def block_at(at):
        return stacked[:, at * LANES : (at + 1) * LANES].astype(F32).T

    for p in range(SIDE // 2):
        block = block_at(p)
        for k in range(2):
            row = (p + k * SIDE // 2) * PLANE
            turned[row : row + MAJOR, :] = block[k * MAJOR : (k + 1) * MAJOR]
    for p in range(SIDE // 4):
        block = block_at(SIDE // 2 + p)
        for k in range(4):
            row = (p + k * SIDE // 4) * PLANE + MAJOR
            turned[row : row + MINOR, :] = block[k * MINOR : (k + 1) * MINOR]
    turned[SIDE * PLANE :, :] = block_at(3 * SIDE // 4)[:PLANE]
    base = core * ROWS
    for i in range(ROWS):
        rows = turned[pl.ds(base + i, SIDE, stride=PLANE), :]
        out[i * SIDE : (i + 1) * SIDE, :] = rows.astype(BF16)
    start = pl.multiple_of(SIDE * PLANE + base, 8)
    out_mask[...] = turned[pl.ds(start, ROWS), :].astype(BF16)
    stack_far(*fars, right, wide)
    for copy in copies:
        copy.wait()


def arrange_left(parts, fars, own, near):
    vmem, anywhere = (pl.BlockSpec(memory_space=m) for m in (pltpu.VMEM, pl.ANY))
    return pl.pallas_call(
        left_kernel,
        in_specs=[vmem] * (len(parts) + len(fars)) + [anywhere] * 2,
        out_specs=[vmem] * 3,
        out_shape=[
            jax.ShapeDtypeStruct((ROWS * SIDE, TOTAL), BF16),
            jax.ShapeDtypeStruct((ROWS, TOTAL), BF16),
            pltpu.VMEM((TOTAL, RIGHT), BF16),
        ],
        scratch_shapes=[
            pltpu.VMEM((TOTAL, LEFT), BF16),
            pltpu.VMEM(((SIDE + 1) * PLANE, TOTAL), F32),
            pltpu.VMEM((CHIP, 2 * COLS), F32),
            pltpu.SemaphoreType.DMA((2,)),
        ],
        compiler_params=pltpu.CompilerParams(vmem_limit_bytes=16 * MEGA),
    )(*parts, *fars, own, near)


def pair_kernel(block, beside, left, left_mask, weight, right, out, outer, scale):
    @pl.when(pl.program_id(0) == 0)
    def _():
        counts = jnp.dot(left_mask[...], right[:, SIDE * COLS :], preferred_element_type=F32)
        scale[...] = 1.0 / (counts + 0.001)

    value = left[...]
    for q in range(SIDE):
        part = jnp.dot(
            value, right[:, q * COLS : (q + 1) * COLS], preferred_element_type=F32
        ).astype(BF16)
        for i in range(block):
            at = i % beside * COLS
            outer[i // beside, q * SIDE : (q + 1) * SIDE, at : at + COLS] = part[
                i * SIDE : (i + 1) * SIDE
            ]
    first = pl.multiple_of(pl.program_id(0) * block, block)
    scales = scale[pl.ds(first, block), :]
    for i in range(0, block, beside):
        projected = jnp.dot(weight[...], outer[i // beside], preferred_element_type=F32)
        for k in range(beside):
            value = projected[:, k * COLS : (k + 1) * COLS] * scales[i + k : i + k + 1]
            out[i + k] = value.T.astype(BF16)


def pair(left, left_mask, weight, right):
    block, beside = 16, 2
    whole = lambda a: pl.BlockSpec(a.shape, lambda i: (0,) * a.ndim)
    return pl.pallas_call(
        functools.partial(pair_kernel, block, beside),
        grid=(ROWS // block,),
        in_specs=[
            pl.BlockSpec((block * SIDE, TOTAL), lambda i: (i, 0)),
            whole(left_mask),
            whole(weight),
            pl.BlockSpec(memory_space=pltpu.VMEM),
        ],
        out_specs=pl.BlockSpec((block, COLS, PAIR), lambda i: (i, 0, 0)),
        out_shape=jax.ShapeDtypeStruct((ROWS, COLS, PAIR), BF16),
        scratch_shapes=[
            pltpu.VMEM((block // beside, SIDE * SIDE, beside * COLS), BF16),
            pltpu.VMEM((ROWS, COLS), F32),
        ],
        compiler_params=pltpu.CompilerParams(vmem_limit_bytes=40 * MEGA),
    )(left, left_mask, weight, right)


def local(
    homolog_embedding,
    sequence_row_mask,
    residue_chain_index,
    standardize_factor,
    standardize_shift,
    first_projector_matrix,
    second_projector_matrix,
    output_weight,
):
    own = project(
        homolog_embedding,
        sequence_row_mask,
        residue_chain_index,
        standardize_factor,
        standardize_shift,
        first_projector_matrix,
        second_projector_matrix,
    )
    along_y = [own[0]] + [res_shift(own[d], 0, d, 0) for d in range(1, RING)]
    far = res_shift(own[RING], 2, 0, 0)
    weight = arrange_weight(output_weight)
    along_y[2], weight = lax.optimization_barrier((along_y[2], weight))
    along_y[3], far = lax.optimization_barrier((along_y[3], far))
    swapped = [core_swap(part) for part in along_y]
    right, left = stack(along_y + swapped)
    left_parts = [to_row_owner(left, k) for k in range(2)]
    near = both_ways(right, 1, 0)
    far_chip = stack_chip(far, core_swap(far), left)
    far_parts = [both_ways(far_chip, 0, 1), res_shift(far, 0, 2, 0)]
    left_parts, far_parts, near = lax.optimization_barrier((left_parts, far_parts, near))
    left_others = [core_swap(part) for part in left_parts]
    far_others = [core_swap(part) for part in far_parts]
    left_others, far_others, near = lax.optimization_barrier((left_others, far_others, near))
    far_parts = [far_chip, far_parts[0], far_others[0], far_parts[1], far_others[1]]
    left_parts = left_parts + left_others
    left_all, left_mask, right_all = arrange_left(left_parts, far_parts, right, near)
    right_all = finish_right(core_swap(near), right_all)
    return pair(left_all, left_mask, weight, right_all)


def solution(mesh):
    in_specs = (P("res", "col", None), P("res", None), P("col"), P(), P(), P(), P(), P())
    out_specs = P("res", "col", None)
    return jax.shard_map(local, mesh=mesh, in_specs=in_specs, out_specs=out_specs, check_vma=False)
```
